1024 devices in a mesh: grp: 16 (over x, y), own: 64 (over z, core).
Axes of the slice: x: 4, y: 4, z: 32, core: 2. Of those that a mesh axis runs over, the one named last changes fastest.
Arguments:
- user_factors: bfloat16 [4194304, 128], P(('grp', 'own')), as said below
- user_rows: int32 [6291456], P(('grp', 'own')), may hold values from 0 to 4095
- row_counts: int32 [1048576], P(('grp', 'own')), may hold values from 1 to 6, as said below
- confidence: bfloat16 [6291456], P(('grp', 'own')), may hold values from 50 to 1000
- slot_items: int32 [1024], replicated, may hold values from 0 to 1023, each once
- prev_factors: float32 [64, 16, 128], P('own', 'grp'), may hold values from -6 to 6
Outputs:
- item_factors: float32 [64, 16, 128], P('own', 'grp')
The draws below stay inside these ranges and needn't reach their ends.
Inputs may be any that keep to these rules, and one draw needn't show every extreme that they name: `user_factors`: each device holds a block of user factor rows; rows and columns differ in scale. `user_rows`: a local row of the same device's block of 4096 users; slots at or beyond the item's count are not used. `row_counts`: some items use all 6 slots on every device.
All inputs are finite; a program needn't handle non-finite values.
Results may differ from the reference program's by a relative error of at most 0.0003.
The reference program's roundings to bfloat16 on the way count: a program that leaves them out, or rounds other values in their place, can miss the bound.
Values may be sent and summed in bfloat16 or wider, within the bound.
A program may use at most 32 MiB of HBM per device.

```python
import math
import jax
import jax.numpy as jnp
from jax import lax

RANK = 128
SLOTS = 6
USERS_DEV = 4096
CG_STEPS = 3
ITEM_OWN = 16
WINDOW = 1024
USERS = 4194304
BLOCKS = 1048576
N_GRP = 16
N_OWN = 64


def draw_user_factors(key, part):
    key = jax.random.fold_in(key, 5)
    keys = jax.random.split(key, 6)
    columns = jnp.exp(jax.random.uniform(keys[0], (RANK,), jnp.float32) * math.log(16.0))
    mix_one = jax.random.uniform(keys[1], (RANK,), jnp.float32, -1.0, 1.0)
    mix_two = jax.random.uniform(keys[2], (RANK,), jnp.float32, -1.0, 1.0)
    common = jax.random.normal(keys[3], (USERS, 2), jnp.float32)
    row_scale = jnp.exp(jax.random.uniform(keys[5], (USERS,), jnp.float32) * math.log(10.0))
    noise = jax.random.normal(keys[4], (USERS, RANK), jnp.float32)
    sigma = (0.1 / USERS) ** 0.5
    values = noise + mix_one[None, :] * common[:, 0:1] + mix_two[None, :] * common[:, 1:2]
    values = sigma * row_scale[:, None] * columns[None, :] * values
    return values.astype(jnp.bfloat16)


def draw_row_counts(key, part):
    key = jax.random.fold_in(key, 11)
    keys = jax.random.split(key, 2)
    order = jax.random.permutation(keys[0], WINDOW)
    popular = order < WINDOW // 8
    base = jax.random.randint(keys[1], (BLOCKS // WINDOW, WINDOW), 1, SLOTS + 1, jnp.int32)
    counts = jnp.where(popular[None, :], SLOTS, base)
    return counts.reshape(BLOCKS).astype(jnp.int32)


def touch_ends(values, stream_key, low, largest):
    extent = values.shape
    index_at = [jax.random.randint(jax.random.fold_in(stream_key, axis), (), 0, extent[axis]) for axis in range(len(extent))]
    values = values.at[tuple(index_at)].set(low)
    longest = extent.index(max(extent))
    index_at[longest] = (index_at[longest] + 1) % extent[longest]
    return values.at[tuple(index_at)].set(largest)


def level_of(own_key, shape, cuts, least, largest):
    factor_of, own = 1.0, jax.random.fold_in(own_key, 6)
    for axis_at, parts in cuts:
        steps = jnp.exp(jax.random.uniform(jax.random.fold_in(own, axis_at), (parts,), jnp.float32, least / len(cuts), largest / len(cuts)))
        factor_of = factor_of * jnp.repeat(steps, shape[axis_at] // parts).reshape([-1 if axis == axis_at else 1 for axis in range(len(shape))])
    return factor_of


def scatter_about(own_key, extent, spread, limit, pieces=(), held_as=jnp.bfloat16):
    values = spread * jax.random.normal(own_key, extent, jnp.float32)
    if pieces:
        values = values * level_of(own_key, extent, pieces, -0.22, 0.18)
    return jnp.clip(values, -limit, limit).astype(held_as)


def setup_inputs(seed: int = 0) -> dict:
    key_of = jax.random.split(jax.random.key(seed), 7)
    return {
        "user_factors": draw_user_factors(jax.random.fold_in(key_of[6], 71), 0),
        "user_rows": touch_ends(jax.random.randint(key_of[1], (BLOCKS * SLOTS,), 0, USERS_DEV), jax.random.fold_in(key_of[1], 1), 0, USERS_DEV - 1).astype(jnp.int32),
        "row_counts": draw_row_counts(jax.random.fold_in(key_of[6], 71), 0),
        "confidence": jnp.clip(jnp.exp(math.log(1000.0) - 2.9957323 * jax.random.uniform(key_of[3], (BLOCKS * SLOTS,), jnp.float32) ** level_of(key_of[3], (BLOCKS * SLOTS,), ((0, 1024),), -0.2, 0.2)), 50.0, 1000.0).astype(jnp.bfloat16),
        "slot_items": jax.random.permutation(key_of[4], WINDOW).astype(jnp.int32),
        "prev_factors": scatter_about(key_of[5], (N_OWN, ITEM_OWN, RANK), 1.0, 6.0, ((0, 64), (1, 16)), jnp.float32),
    }


RIDGE = 4.0
EPSILON = 1e-6


def conjugate(system, rhs, start):
    def applied_to(vector):
        return jnp.einsum('ikl,il->ik', system, vector, precision=lax.Precision.HIGHEST)

    answer = start
    residual = rhs - applied_to(start)
    direction = residual
    norm_now = jnp.sum(residual * residual, axis=1)
    for step in range(CG_STEPS):
        applied = applied_to(direction)
        step_size = norm_now / (jnp.sum(direction * applied, axis=1) + EPSILON)
        answer = answer + step_size[:, None] * direction
        residual = residual - step_size[:, None] * applied
        norm_next = jnp.sum(residual * residual, axis=1)
        direction = residual + (norm_next / (norm_now + EPSILON))[:, None] * direction
        norm_now = norm_next
    return answer


def reference(user_factors, user_rows, row_counts, confidence, slot_items, prev_factors):
    blocks = N_GRP * N_OWN
    user_gram = jnp.dot(user_factors.T, user_factors, preferred_element_type=jnp.float32)
    offsets = jnp.arange(blocks, dtype=jnp.int32) * USERS_DEV
    index_all = user_rows.reshape(blocks, WINDOW, SLOTS) + offsets[:, None, None]
    count_all = row_counts.reshape(blocks, WINDOW)
    weight_all = confidence.reshape(blocks, WINDOW, SLOTS)
    starts = prev_factors.reshape(WINDOW, RANK)
    positions = jnp.arange(SLOTS, dtype=jnp.int32)
    identity = jnp.eye(RANK, dtype=jnp.float32)

    def one_slot(slot):
        item = slot_items[slot]
        picked = jnp.take(index_all, item, axis=1).reshape(-1)
        factor_rows = jnp.take(user_factors, picked, axis=0)
        is_live = (positions[None, :] < jnp.take(count_all, item, axis=1)[:, None]).reshape(-1)
        factor_rows = jnp.where(is_live[:, None], factor_rows, jnp.zeros_like(factor_rows))
        conf_values = jnp.take(weight_all, item, axis=1).reshape(-1).astype(jnp.float32)
        scaled = (conf_values[:, None] * factor_rows.astype(jnp.float32)).astype(jnp.bfloat16)
        weight = (1.0 + conf_values).astype(jnp.bfloat16)
        item_gram = jnp.dot(scaled.T, factor_rows, preferred_element_type=jnp.float32)
        rhs = jnp.dot(weight, factor_rows, preferred_element_type=jnp.float32)
        system = user_gram + item_gram + RIDGE * identity
        return conjugate(system[None], rhs[None], starts[slot][None])[0]

    result = lax.map(one_slot, jnp.arange(WINDOW, dtype=jnp.int32))
    return result.reshape(N_OWN, ITEM_OWN, RANK)
```

```python
import functools

import jax
import jax.numpy as jnp
from jax import lax
from jax.experimental import pallas as pl
from jax.experimental.pallas import tpu as pltpu
from jax.sharding import PartitionSpec as P

CG_STEPS = 3
RIDGE = 4.0
EPSILON = 1e-06

RANK = 128
DEPTH = 6
USERS = 4096
WINDOW = 1024
SIDE = 4
PLANES = 32
PEERS = 32
CHUNKS = 4
GROUP = PLANES // CHUNKS
STEPS = PLANES // 2
ROWS = GROUP * DEPTH
HALF = RANK // 2
BODY = RANK
UNIT = 136
SLICE = 8
MESH = pl.DeviceIdType.MESH


def place():
    grp = lax.axis_index("grp")
    own = lax.axis_index("own")
    return grp // SIDE, grp % SIDE, own // 2, own % 2


def peer(step):
    gx, gy, z, core = place()
    px = (gx + (step // 2) % SIDE) % SIDE
    py = (gy + step // (2 * SIDE)) % SIDE
    pc = (core + step % 2) % 2
    grp = px * SIDE + py
    return pc * 16 + grp, (grp, z * 2 + pc)


def neighbour(step):
    _, _, z, core = place()
    return (lax.axis_index("grp"), ((z + step + PLANES) % PLANES) * 2 + core)


def plane_of(chunk, index):
    z = lax.axis_index("own") // 2
    step = chunk * (GROUP // 2) + index // 2
    away = STEPS - step if index % 2 == 0 else step - (STEPS - 1)
    return (z + away + PLANES) % PLANES


def solve(system, rhs, start):
    row = lax.broadcasted_iota(jnp.int32, (RANK, RANK), 0)
    col = lax.broadcasted_iota(jnp.int32, (RANK, RANK), 1)
    same = row == col

    def applied_to(vector):
        column = jnp.sum(system * vector, axis=1, keepdims=True)
        return jnp.sum(jnp.where(same, column, 0.0), axis=0, keepdims=True)

    answer = start
    residual = rhs - applied_to(start)
    direction = residual
    norm_now = jnp.sum(residual * residual, axis=1, keepdims=True)
    for step in range(CG_STEPS):
        applied = applied_to(direction)
        step_size = norm_now / (jnp.sum(direction * applied, axis=1, keepdims=True) + EPSILON)
        answer = answer + step_size * direction
        residual = residual - step_size * applied
        norm_next = jnp.sum(residual * residual, axis=1, keepdims=True)
        direction = residual + (norm_next / (norm_now + EPSILON)) * direction
        norm_now = norm_next
    return answer


def kernel(
    items, rows, conf, users, start, out,
    wide, stage, send, recv, flat, conf_wide, conf_stage, conf_send, conf_recv, conf_all, weight_all,
    gram_own, gram_pair, gram_parts, gram_piece, gram_sum, gram_pack, up_send, up_recv, down_send, down_recv,
    send_sem, recv_sem, self_sem, conf_send_sem, conf_recv_sem, conf_self_sem, pair_sem, part_sem, sum_sem,
    up_send_sem, up_recv_sem, down_send_sem, down_recv_sem,
):
    gx, gy, z, core = place()
    grp = gx * SIDE + gy
    me = core * 16 + grp
    barrier = pltpu.get_barrier_semaphore()

    def greet(step, carry):
        pl.semaphore_signal(barrier, inc=1, device_id=peer(step)[1], device_id_type=MESH)
        return carry

    lax.fori_loop(1, PEERS, greet, 0)
    for step in (1, -1):
        pl.semaphore_signal(barrier, inc=1, device_id=neighbour(step), device_id_type=MESH)

    gram_own[...] = jnp.zeros_like(gram_own)

    def own_gram(block, carry):
        at = pl.ds(pl.multiple_of(block * 512, 512), 512)
        part = users[at, :]
        wide[at, :] = part.astype(jnp.float32)
        gram_own[...] += lax.dot_general(part, part, (((0,), (0,)), ((), ())), preferred_element_type=jnp.float32)
        return carry

    lax.fori_loop(0, USERS // 512, own_gram, 0)

    spread_row = lax.broadcasted_iota(jnp.int32, (8, RANK), 0)
    spread_col = lax.broadcasted_iota(jnp.int32, (8, RANK), 1)
    mine = (spread_col // 8) % 8 == me % 8
    spread = jnp.where(jnp.logical_and(mine, spread_col % 8 == spread_row), 1.0, 0.0).astype(jnp.bfloat16)
    conf_wide[...] = jnp.dot(conf[...], spread, preferred_element_type=jnp.float32)

    for index in range(16):
        flat[pl.ds(index * 128, 128), :] = jnp.zeros((128, RANK), jnp.float32)

    pl.semaphore_wait(barrier, PEERS + 1)

    pair = pltpu.make_async_remote_copy(
        src_ref=gram_own, dst_ref=gram_pair, send_sem=pair_sem.at[0], recv_sem=pair_sem.at[1],
        device_id=(grp, z * 2 + (1 - core)), device_id_type=MESH,
    )
    pair.start()

    def gather(chunk):
        planes = [plane_of(chunk, index) for index in range(GROUP)]

        def owner(to, carry):
            for index in range(GROUP):
                item = items[planes[index] * PEERS + to]
                for slot in range(DEPTH):
                    row = rows[item * DEPTH + slot]
                    stage[pl.ds(to * ROWS + slot * GROUP + index, 1), :] = wide[pl.ds(row, 1), :]
                conf_stage[pl.ds(to * PLANES + chunk * GROUP + index, 1), :] = conf_wide[pl.ds(item, 1), :]
            return carry

        lax.fori_loop(0, PEERS, owner, 0)

        def narrow(block, carry):
            at = pl.ds(pl.multiple_of(block * ROWS * 4, ROWS * 4), ROWS * 4)
            part = stage[at, :].astype(jnp.bfloat16)
            send[chunk, pl.ds(block * 4, 4)] = part.reshape(4, ROWS, RANK)
            return carry

        lax.fori_loop(0, PEERS // 4, narrow, 0)

    def post(chunk):
        def one(step, carry):
            to, device = peer(step)
            pltpu.make_async_remote_copy(
                src_ref=send.at[chunk, to], dst_ref=recv.at[chunk, me], send_sem=send_sem.at[chunk],
                recv_sem=recv_sem.at[chunk], device_id=device, device_id_type=MESH,
            ).start()
            return carry

        lax.fori_loop(1, PEERS, one, 0)
        pltpu.make_async_copy(send.at[chunk, me], recv.at[chunk, me], self_sem.at[chunk]).start()

    def post_conf():
        left = lax.broadcasted_iota(jnp.int32, (16, RANK), 1) < HALF

        def narrow(to, carry):
            first = conf_stage[pl.ds(to * PLANES, 16), :]
            second = conf_stage[pl.ds(to * PLANES + 16, 16), :]
            conf_send[to] = jnp.where(left, first, second).astype(jnp.bfloat16)
            return carry

        lax.fori_loop(0, PEERS, narrow, 0)

        def one(step, carry):
            to, device = peer(step)
            pltpu.make_async_remote_copy(
                src_ref=conf_send.at[to], dst_ref=conf_recv.at[me], send_sem=conf_send_sem,
                recv_sem=conf_recv_sem, device_id=device, device_id_type=MESH,
            ).start()
            return carry

        lax.fori_loop(1, PEERS, one, 0)
        pltpu.make_async_copy(conf_send.at[me], conf_recv.at[me], conf_self_sem).start()

    def take_conf():
        pltpu.make_async_copy(
            conf_recv.at[pl.ds(0, PEERS - 1)], conf_recv.at[pl.ds(0, PEERS - 1)], conf_recv_sem
        ).wait()
        pltpu.make_async_copy(conf_send.at[me], conf_recv.at[me], conf_self_sem).wait()
        left = lax.broadcasted_iota(jnp.int32, (16, RANK), 1) < HALF
        sums = []
        for part in range(4):
            total = jnp.zeros((16, RANK), jnp.float32)
            for index in range(8):
                total = total + conf_recv[part * 8 + index].astype(jnp.float32)
            sums.append(total)
        for part in range(2):
            one, two = sums[2 * part], sums[2 * part + 1]
            first = jnp.where(left, one, pltpu.roll(two, HALF, 1))
            second = jnp.where(left, pltpu.roll(one, HALF, 1), two)
            at = pl.ds(part * RANK, RANK)
            conf_all[pl.ds(0, 16), at] = first
            conf_all[pl.ds(16, 16), at] = second
        values = conf_all[...]
        weight = (1.0 + values).astype(jnp.bfloat16).astype(jnp.float32)
        weight_all[...] = jnp.where(values > 0.0, weight, 0.0)

    def sum_pair():
        pair.wait()
        gram_own[...] += gram_pair[...]

    def post_parts():
        def one(step, carry):
            px = (gx + step % SIDE) % SIDE
            py = (gy + step // SIDE) % SIDE
            to = px * SIDE + py
            pltpu.make_async_remote_copy(
                src_ref=gram_own.at[pl.ds(to * SLICE, SLICE)], dst_ref=gram_parts.at[grp], send_sem=part_sem.at[0],
                recv_sem=part_sem.at[1], device_id=(to, z * 2 + core), device_id_type=MESH,
            ).start()
            return carry

        lax.fori_loop(1, 16, one, 0)
        gram_parts[grp] = gram_own[pl.ds(pl.multiple_of(grp * SLICE, SLICE), SLICE), :]

    def wait_fifteen(ref, sem):
        pltpu.make_async_copy(ref.at[pl.ds(0, 15)], ref.at[pl.ds(0, 15)], sem).wait()

    def post_sums():
        wait_fifteen(gram_parts, part_sem.at[1])
        total = gram_parts[0]
        for index in range(1, 16):
            total = total + gram_parts[index]
        gram_piece[...] = total

        def one(step, carry):
            px = (gx + step % SIDE) % SIDE
            py = (gy + step // SIDE) % SIDE
            to = px * SIDE + py
            pltpu.make_async_remote_copy(
                src_ref=gram_piece, dst_ref=gram_sum.at[grp], send_sem=sum_sem.at[0],
                recv_sem=sum_sem.at[1], device_id=(to, z * 2 + core), device_id_type=MESH,
            ).start()
            return carry

        lax.fori_loop(1, 16, one, 0)
        gram_sum[grp] = total

    def take_sums():
        wait_fifteen(gram_sum, sum_sem.at[1])
        gram_pack[pl.ds(0, BODY), :] = gram_sum[...].reshape(RANK, RANK)
        gram_pack[pl.ds(BODY, 8), :] = jnp.zeros((8, RANK), jnp.float32)

    def item_pack(into, chunk, index):
        values = flat[pl.ds(index, PEERS * 8, stride=GROUP), :]
        conf_row = conf_all[pl.ds(chunk * GROUP + index, 1), :]
        weight = weight_all[pl.ds(chunk * GROUP + index, 1), :]
        scaled = (jnp.transpose(values) * conf_row).astype(jnp.bfloat16)
        weights = jnp.broadcast_to(weight, (16, PEERS * 8)).astype(jnp.bfloat16)
        left = jnp.concatenate([scaled, weights], axis=0)
        product = jnp.dot(left, values.astype(jnp.bfloat16), preferred_element_type=jnp.float32)
        into[pl.ds(0, BODY), :] = product[:BODY] + gram_pack[pl.ds(0, BODY), :]
        into[pl.ds(BODY, 8), :] = product[BODY:BODY + 8]

    def up_copy(step):
        return pltpu.make_async_remote_copy(
            src_ref=up_send.at[step], dst_ref=up_recv.at[step], send_sem=up_send_sem.at[step],
            recv_sem=up_recv_sem.at[step], device_id=neighbour(1), device_id_type=MESH,
        )

    def down_copy(step):
        return pltpu.make_async_remote_copy(
            src_ref=down_send.at[step], dst_ref=down_recv.at[step], send_sem=down_send_sem.at[step],
            recv_sem=down_recv_sem.at[step], device_id=neighbour(-1), device_id_type=MESH,
        )

    gather(0)
    post(0)
    sum_pair()
    post_parts()
    gather(1)
    post(1)
    post_sums()
    gather(2)
    post(2)
    gather(3)
    post_conf()
    post(3)
    take_sums()
    take_conf()

    def chain(step, carry):
        chunk = step // (GROUP // 2)
        index = (step % (GROUP // 2)) * 2

        @pl.when(index == 0)
        def _():
            pltpu.make_async_copy(
                recv.at[chunk, pl.ds(0, PEERS - 1)], recv.at[chunk, pl.ds(0, PEERS - 1)], recv_sem.at[chunk]
            ).wait()
            pltpu.make_async_copy(send.at[chunk, me], recv.at[chunk, me], self_sem.at[chunk]).wait()

            def widen(source, carry):
                at = pl.ds(pl.multiple_of(source * 64, 64), ROWS)
                flat[at, :] = recv[chunk, source].astype(jnp.float32)
                return carry

            lax.fori_loop(0, PEERS, widen, 0)

        item_pack(up_send.at[step], chunk, index)
        item_pack(down_send.at[step], chunk, index + 1)

        @pl.when(step > 0)
        def _():
            up_copy(step - 1).wait_recv()
            up_send[step] += up_recv[step - 1]
            down_copy(step - 1).wait_recv()
            down_send[step] += down_recv[step - 1]

        up_copy(step).start()

        @pl.when(step < STEPS - 1)
        def _():
            down_copy(step).start()

        return carry

    lax.fori_loop(0, STEPS, chain, 0)
    up_copy(STEPS - 1).wait_recv()
    total = down_send[STEPS - 1] + up_recv[STEPS - 1]
    row = lax.broadcasted_iota(jnp.int32, (RANK, RANK), 0)
    col = lax.broadcasted_iota(jnp.int32, (RANK, RANK), 1)
    system = total[:BODY] + jnp.where(row == col, RIDGE, 0.0)
    out[0] = solve(system, total[BODY:BODY + 1], start[0])

    for chunk in range(CHUNKS):
        pltpu.make_async_copy(
            send.at[chunk, pl.ds(0, PEERS - 1)], send.at[chunk, pl.ds(0, PEERS - 1)], send_sem.at[chunk]
        ).wait()
    pltpu.make_async_copy(
        conf_send.at[pl.ds(0, PEERS - 1)], conf_send.at[pl.ds(0, PEERS - 1)], conf_send_sem
    ).wait()
    wait_fifteen(gram_parts, part_sem.at[0])
    wait_fifteen(gram_sum, sum_sem.at[0])

    def drain(step, carry):
        up_copy(step).wait_send()

        @pl.when(step < STEPS - 1)
        def _():
            down_copy(step).wait_send()

        return carry

    lax.fori_loop(0, STEPS, drain, 0)


def on_device(user_factors, user_rows, row_counts, confidence, slot_items, prev_factors):
    conf = confidence.reshape(WINDOW, DEPTH)
    live = lax.broadcasted_iota(jnp.int32, (WINDOW, DEPTH), 1) < row_counts[:, None]
    conf = jnp.pad(jnp.where(live, conf, jnp.zeros_like(conf)), ((0, 0), (0, 8 - DEPTH)))
    vmem = pl.BlockSpec(memory_space=pltpu.VMEM)
    smem = pl.BlockSpec(memory_space=pltpu.SMEM)
    f32, bf16 = jnp.float32, jnp.bfloat16
    dma = pltpu.SemaphoreType.DMA
    return pl.pallas_call(
        kernel,
        out_shape=jax.ShapeDtypeStruct((1, 1, RANK), f32),
        in_specs=[smem, smem, vmem, vmem, vmem],
        out_specs=vmem,
        scratch_shapes=[
            pltpu.VMEM((USERS, RANK), f32),
            pltpu.VMEM((PEERS * ROWS, RANK), f32),
            pltpu.VMEM((CHUNKS, PEERS, ROWS, RANK), bf16),
            pltpu.VMEM((CHUNKS, PEERS, ROWS, RANK), bf16),
            pltpu.VMEM((PEERS * 8 * GROUP, RANK), f32),
            pltpu.VMEM((WINDOW, RANK), f32),
            pltpu.VMEM((WINDOW, RANK), f32),
            pltpu.VMEM((PEERS, 16, RANK), bf16),
            pltpu.VMEM((PEERS, 16, RANK), bf16),
            pltpu.VMEM((PLANES, PEERS * 8), f32),
            pltpu.VMEM((PLANES, PEERS * 8), f32),
            pltpu.VMEM((RANK, RANK), f32),
            pltpu.VMEM((RANK, RANK), f32),
            pltpu.VMEM((16, SLICE, RANK), f32),
            pltpu.VMEM((SLICE, RANK), f32),
            pltpu.VMEM((16, SLICE, RANK), f32),
            pltpu.VMEM((UNIT, RANK), f32),
            pltpu.VMEM((STEPS, UNIT, RANK), f32),
            pltpu.VMEM((STEPS, UNIT, RANK), f32),
            pltpu.VMEM((STEPS, UNIT, RANK), f32),
            pltpu.VMEM((STEPS, UNIT, RANK), f32),
            dma((CHUNKS,)), dma((CHUNKS,)), dma((CHUNKS,)), dma, dma, dma, dma((2,)), dma((2,)), dma((2,)),
            dma((STEPS,)), dma((STEPS,)), dma((STEPS,)), dma((STEPS,)),
        ],
        compiler_params=pltpu.CompilerParams(
            collective_id=0, has_side_effects=True, vmem_limit_bytes=48 * 1024 * 1024
        ),
    )(slot_items, user_rows, conf, user_factors, prev_factors)


def solution(mesh):
    in_specs = (
        P(("grp", "own"), None),
        P(("grp", "own")),
        P(("grp", "own")),
        P(("grp", "own")),
        P(),
        P("own", "grp", None),
    )
    out_specs = P("own", "grp", None)
    return jax.shard_map(
        on_device, mesh=mesh, in_specs=in_specs, out_specs=out_specs, check_vma=False
    )
```

```python
import jax
import jax.numpy as jnp
from jax import lax
from jax.experimental import pallas as pl
from jax.experimental.pallas import tpu as pltpu
from jax.sharding import PartitionSpec as P

CG_STEPS = 3
RIDGE = 4.0
EPSILON = 1e-06

RANK = 128
DEPTH = 6
USERS = 4096
WINDOW = 1024
SIDE = 4
PLANES = 32
PLANE = 32
PEERS = 2 * PLANE
ITEMS = WINDOW // PEERS
CHUNKS = 2
GROUP = ITEMS // CHUNKS
STEPS = ITEMS // 2
ROWS = GROUP * DEPTH
PADDED = 8
LENGTH = PEERS * PADDED
UNIT = RANK + 8
CUTS = ((0, 32), (32, 32), (64, 32), (96, 40))
PIECE = RANK // PLANE
MESH = pl.DeviceIdType.MESH


def place():
    grp = lax.axis_index("grp")
    own = lax.axis_index("own")
    return grp // SIDE, grp % SIDE, own // 2, own % 2


def other_plane(z, core):
    odd = z % 2
    away = 1 - 2 * odd
    return (z + away * (1 - 2 * core) + PLANES) % PLANES


def peer(step):
    gx, gy, _, core = place()
    px = (gx + (step // 2) % SIDE) % SIDE
    py = (gy + step // (2 * SIDE)) % SIDE
    pc = (core + step % 2) % 2
    grp = px * SIDE + py
    return grp, pc, pc * 16 + grp


def along(step):
    _, _, z, core = place()
    return (lax.axis_index("grp"), ((z + step + PLANES) % PLANES) * 2 + core)


def solve(system, rhs, start):
    row = lax.broadcasted_iota(jnp.int32, (RANK, RANK), 0)
    col = lax.broadcasted_iota(jnp.int32, (RANK, RANK), 1)
    same = row == col

    def applied_to(vector):
        column = jnp.sum(system * vector, axis=1, keepdims=True)
        return jnp.sum(jnp.where(same, column, 0.0), axis=0, keepdims=True)

    answer = start
    residual = rhs - applied_to(start)
    direction = residual
    norm_now = jnp.sum(residual * residual, axis=1, keepdims=True)
    for step in range(CG_STEPS):
        applied = applied_to(direction)
        step_size = norm_now / (jnp.sum(direction * applied, axis=1, keepdims=True) + EPSILON)
        answer = answer + step_size * direction
        residual = residual - step_size * applied
        norm_next = jnp.sum(residual * residual, axis=1, keepdims=True)
        direction = residual + (norm_next / (norm_now + EPSILON)) * direction
        norm_now = norm_next
    return answer


def kernel(
    items, rows, conf, users, start, out,
    wide, stage, send, recv, flat, conf_wide, conf_stage, conf_send, conf_recv, conf_all, weight_all,
    gram_own, gram_cut, gram_parts, gram_piece, gram_planes, gram_total, gram_all,
    up_send, up_recv, down_send, down_recv,
    send_sem, recv_sem, self_sem, conf_send_sem, conf_recv_sem, conf_self_sem, part_sem, plane_sem, all_sem,
    up_send_sem, up_recv_sem, down_send_sem, down_recv_sem,
):
    _, _, z, core = place()
    me = core * 16 + lax.axis_index("grp")
    barrier = pltpu.get_barrier_semaphore()

    def greet(device):
        pl.semaphore_signal(barrier, inc=1, device_id=device, device_id_type=MESH)

    def greet_plane(step, carry):
        grp, pc, _ = peer(step)

        @pl.when(step > 0)
        def _():
            greet((grp, z * 2 + pc))
            greet(along(step))

        greet((grp, other_plane(z, core) * 2 + pc))
        return carry

    lax.fori_loop(0, PLANE, greet_plane, 0)

    def widen_users(block, carry):
        at = pl.ds(pl.multiple_of(block * 512, 512), 512)
        wide[at, :] = users[at, :].astype(jnp.float32)
        return carry

    lax.fori_loop(0, USERS // 512, widen_users, 0)

    def gather(chunk):
        def owner(to, carry):
            d = to % PLANE
            far = other_plane(z, d // 16)
            base = jnp.where(to < PLANE, z, far)
            for index in range(GROUP):
                step = chunk * (GROUP // 2) + index // 2
                away = STEPS - step if index % 2 == 0 else step - (STEPS - 1)
                item = items[((base + 2 * away + PLANES) % PLANES) * PLANE + d]
                for slot in range(DEPTH):
                    row = rows[item * DEPTH + slot]
                    stage[pl.ds(to * ROWS + slot * GROUP + index, 1), :] = wide[pl.ds(row, 1), :]
            return carry

        lax.fori_loop(0, PEERS, owner, 0)

        def narrow(block, carry):
            at = pl.ds(pl.multiple_of(block * ROWS * 4, ROWS * 4), ROWS * 4)
            part = stage[at, :].astype(jnp.bfloat16)
            send[chunk, pl.ds(block * 4, 4)] = part.reshape(4, ROWS, RANK)
            return carry

        lax.fori_loop(0, PEERS // 4, narrow, 0)

    def post(source, target, send_to, recv_from, self_to):
        def one(step, carry):
            grp, pc, d = peer(step)

            @pl.when(step > 0)
            def _():
                pltpu.make_async_remote_copy(
                    src_ref=source(d), dst_ref=target(me), send_sem=send_to, recv_sem=recv_from,
                    device_id=(grp, z * 2 + pc), device_id_type=MESH,
                ).start()

            pltpu.make_async_remote_copy(
                src_ref=source(PLANE + d), dst_ref=target(PLANE + me), send_sem=send_to, recv_sem=recv_from,
                device_id=(grp, other_plane(z, pc) * 2 + pc), device_id_type=MESH,
            ).start()
            return carry

        lax.fori_loop(0, PLANE, one, 0)
        pltpu.make_async_copy(source(me), target(me), self_to).start()

    def wait_blocks(ref, count, sem):
        pltpu.make_async_copy(ref.at[pl.ds(0, count)], ref.at[pl.ds(0, count)], sem).wait()

    def post_rows(chunk):
        post(
            lambda d: send.at[chunk, d], lambda d: recv.at[chunk, d],
            send_sem.at[chunk], recv_sem.at[chunk], self_sem.at[chunk],
        )

    def post_conf():
        spread_row = lax.broadcasted_iota(jnp.int32, (8, RANK), 0)
        spread_col = lax.broadcasted_iota(jnp.int32, (8, RANK), 1)
        mine = spread_col // PADDED == me % 16
        spread = jnp.where(jnp.logical_and(mine, spread_col % PADDED == spread_row), 1.0, 0.0).astype(jnp.bfloat16)
        conf_wide[...] = jnp.dot(conf[...], spread, preferred_element_type=jnp.float32)

        def owner(to, carry):
            d = to % PLANE
            far = other_plane(z, d // 16)
            base = jnp.where(to < PLANE, z, far)
            for index in range(ITEMS):
                step = index // 2
                away = STEPS - step if index % 2 == 0 else step - (STEPS - 1)
                item = items[((base + 2 * away + PLANES) % PLANES) * PLANE + d]
                conf_stage[pl.ds(to * ITEMS + index, 1), :] = conf_wide[pl.ds(item, 1), :]
            return carry

        lax.fori_loop(0, PEERS, owner, 0)

        def narrow(block, carry):
            at = pl.ds(pl.multiple_of(block * ITEMS * 8, ITEMS * 8), ITEMS * 8)
            conf_send[pl.ds(block * 8, 8)] = conf_stage[at, :].astype(jnp.bfloat16).reshape(8, ITEMS, RANK)
            return carry

        lax.fori_loop(0, PEERS // 8, narrow, 0)
        post(lambda d: conf_send.at[d], lambda d: conf_recv.at[d], conf_send_sem, conf_recv_sem, conf_self_sem)

    def take_conf():
        wait_blocks(conf_recv, PEERS - 1, conf_recv_sem)
        pltpu.make_async_copy(conf_send.at[me], conf_recv.at[me], conf_self_sem).wait()
        for part in range(PEERS // 16):
            total = jnp.zeros((ITEMS, RANK), jnp.float32)
            for index in range(16):
                total = total + conf_recv[part * 16 + index].astype(jnp.float32)
            conf_all[:, pl.ds(part * RANK, RANK)] = total
        values = conf_all[...]
        weight = (1.0 + values).astype(jnp.bfloat16).astype(jnp.float32)
        weight_all[...] = jnp.where(values > 0.0, weight, 0.0)

    def post_gram():
        gram_own[...] = jnp.zeros_like(gram_own)

        def one_block(block, carry):
            part = users[pl.ds(pl.multiple_of(block * 512, 512), 512), :]
            gram_own[...] += lax.dot_general(part, part, (((0,), (0,)), ((), ())), preferred_element_type=jnp.float32)
            return carry

        lax.fori_loop(0, USERS // 512, one_block, 0)
        for index in range(PLANE):
            gram_cut[index] = gram_own[pl.ds(index * PIECE, PIECE), :]

        def one(step, carry):
            grp, pc, d = peer(step)
            pltpu.make_async_remote_copy(
                src_ref=gram_cut.at[d], dst_ref=gram_parts.at[me], send_sem=part_sem.at[0],
                recv_sem=part_sem.at[1], device_id=(grp, z * 2 + pc), device_id_type=MESH,
            ).start()
            return carry

        lax.fori_loop(1, PLANE, one, 0)
        gram_parts[me] = gram_cut[me]

    def post_piece():
        wait_blocks(gram_parts, PLANE - 1, part_sem.at[1])
        total = jnp.sum(gram_parts[...], axis=0)
        gram_piece[...] = total

        def one(step, carry):
            pltpu.make_async_remote_copy(
                src_ref=gram_piece, dst_ref=gram_planes.at[z], send_sem=plane_sem.at[0],
                recv_sem=plane_sem.at[1], device_id=along(step), device_id_type=MESH,
            ).start()
            return carry

        lax.fori_loop(1, PLANES, one, 0)
        gram_planes[z] = total

    def post_total():
        wait_blocks(gram_planes, PLANES - 1, plane_sem.at[1])
        total = jnp.sum(gram_planes[...], axis=0)
        gram_total[...] = total

        def one(step, carry):
            grp, pc, d = peer(step)
            pltpu.make_async_remote_copy(
                src_ref=gram_total, dst_ref=gram_all.at[me], send_sem=all_sem.at[0],
                recv_sem=all_sem.at[1], device_id=(grp, z * 2 + pc), device_id_type=MESH,
            ).start()
            return carry

        lax.fori_loop(1, PLANE, one, 0)
        gram_all[me] = total

    def item_gram(into, at, index):
        values = flat[pl.ds(index, LENGTH, stride=GROUP), :]
        scaled = (jnp.transpose(values) * conf_all[pl.ds(at, 1), :]).astype(jnp.bfloat16)
        weights = jnp.broadcast_to(weight_all[pl.ds(at, 1), :], (16, LENGTH)).astype(jnp.bfloat16)
        left = jnp.concatenate([scaled, weights], axis=0)
        product = jnp.dot(left, values.astype(jnp.bfloat16), preferred_element_type=jnp.float32)
        into[...] = product[:UNIT]

    def up_copy(step, part):
        first, count = CUTS[part]
        at = pl.ds(first, count)
        return pltpu.make_async_remote_copy(
            src_ref=up_send.at[step, at], dst_ref=up_recv.at[step, at], send_sem=up_send_sem.at[step, part],
            recv_sem=up_recv_sem.at[step, part], device_id=along(2), device_id_type=MESH,
        )

    def down_copy(step, part):
        first, count = CUTS[part]
        at = pl.ds(first, count)
        return pltpu.make_async_remote_copy(
            src_ref=down_send.at[step, at], dst_ref=down_recv.at[step, at], send_sem=down_send_sem.at[step, part],
            recv_sem=down_recv_sem.at[step, part], device_id=along(-2), device_id_type=MESH,
        )

    for index in range(LENGTH * GROUP // 256):
        flat[pl.ds(index * 256, 256), :] = jnp.zeros((256, RANK), jnp.float32)
    gather(0)
    pl.semaphore_wait(barrier, 2 * (PLANE - 1) + PLANE)
    post_rows(0)
    post_conf()
    post_gram()
    gather(1)
    post_rows(1)
    take_conf()

    def chain(step, carry):
        chunk = step // (GROUP // 2)
        index = (step % (GROUP // 2)) * 2

        @pl.when(index == 0)
        def _():
            pltpu.make_async_copy(
                recv.at[chunk, pl.ds(0, PEERS - 1)], recv.at[chunk, pl.ds(0, PEERS - 1)], recv_sem.at[chunk]
            ).wait()
            pltpu.make_async_copy(send.at[chunk, me], recv.at[chunk, me], self_sem.at[chunk]).wait()

            def widen(source, carry):
                at = pl.ds(pl.multiple_of(source * PADDED * GROUP, PADDED * GROUP), ROWS)
                flat[at, :] = recv[chunk, source].astype(jnp.float32)
                return carry

            lax.fori_loop(0, PEERS, widen, 0)

        item_gram(up_send.at[step], step * 2, index)
        item_gram(down_send.at[step], step * 2 + 1, index + 1)

        for part, (first, count) in enumerate(CUTS):
            at = pl.ds(first, count)

            @pl.when(step > 0)
            def _():
                up_copy(step - 1, part).wait_recv()
                up_send[step, at] += up_recv[step - 1, at]

            up_copy(step, part).start()

            @pl.when(step > 0)
            def _():
                down_copy(step - 1, part).wait_recv()
                down_send[step, at] += down_recv[step - 1, at]

            @pl.when(step < STEPS - 1)
            def _():
                down_copy(step, part).start()

        @pl.when(step == 1)
        def _():
            post_piece()

        @pl.when(step == 4)
        def _():
            post_total()

        return carry

    lax.fori_loop(0, STEPS, chain, 0)
    wait_blocks(gram_all, PLANE - 1, all_sem.at[1])
    row = lax.broadcasted_iota(jnp.int32, (RANK, RANK), 0)
    col = lax.broadcasted_iota(jnp.int32, (RANK, RANK), 1)
    for index in range(PLANE):
        gram_own[pl.ds(index * PIECE, PIECE), :] = gram_all[index]
    gram_own[...] += jnp.where(row == col, RIDGE, 0.0) + down_send[STEPS - 1, pl.ds(0, RANK)]
    for part in range(len(CUTS)):
        up_copy(STEPS - 1, part).wait_recv()
    system = gram_own[...] + up_recv[STEPS - 1, pl.ds(0, RANK)]
    rhs = down_send[STEPS - 1, pl.ds(RANK, 1)] + up_recv[STEPS - 1, pl.ds(RANK, 1)]
    out[0] = solve(system, rhs, start[0])

    for chunk in range(CHUNKS):
        pltpu.make_async_copy(
            send.at[chunk, pl.ds(0, PEERS - 1)], send.at[chunk, pl.ds(0, PEERS - 1)], send_sem.at[chunk]
        ).wait()
    wait_blocks(conf_send, PEERS - 1, conf_send_sem)
    wait_blocks(gram_parts, PLANE - 1, part_sem.at[0])
    wait_blocks(gram_planes, PLANES - 1, plane_sem.at[0])
    wait_blocks(gram_all, PLANE - 1, all_sem.at[0])

    def drain(step, carry):
        for part in range(len(CUTS)):
            up_copy(step, part).wait_send()

            @pl.when(step < STEPS - 1)
            def _():
                down_copy(step, part).wait_send()

        return carry

    lax.fori_loop(0, STEPS, drain, 0)


def on_device(user_factors, user_rows, row_counts, confidence, slot_items, prev_factors):
    conf = confidence.reshape(WINDOW, DEPTH)
    live = lax.broadcasted_iota(jnp.int32, (WINDOW, DEPTH), 1) < row_counts[:, None]
    conf = jnp.pad(jnp.where(live, conf, jnp.zeros_like(conf)), ((0, 0), (0, 8 - DEPTH)))
    vmem = pl.BlockSpec(memory_space=pltpu.VMEM)
    smem = pl.BlockSpec(memory_space=pltpu.SMEM)
    f32, bf16 = jnp.float32, jnp.bfloat16
    dma = pltpu.SemaphoreType.DMA
    parts = len(CUTS)
    return pl.pallas_call(
        kernel,
        out_shape=jax.ShapeDtypeStruct((1, 1, RANK), f32),
        in_specs=[smem, smem, vmem, vmem, vmem],
        out_specs=vmem,
        scratch_shapes=[
            pltpu.VMEM((USERS, RANK), f32),
            pltpu.VMEM((PEERS * ROWS, RANK), f32),
            pltpu.VMEM((CHUNKS, PEERS, ROWS, RANK), bf16),
            pltpu.VMEM((CHUNKS, PEERS, ROWS, RANK), bf16),
            pltpu.VMEM((LENGTH * GROUP, RANK), f32),
            pltpu.VMEM((WINDOW, RANK), f32),
            pltpu.VMEM((WINDOW, RANK), f32),
            pltpu.VMEM((PEERS, ITEMS, RANK), bf16),
            pltpu.VMEM((PEERS, ITEMS, RANK), bf16),
            pltpu.VMEM((ITEMS, LENGTH), f32),
            pltpu.VMEM((ITEMS, LENGTH), f32),
            pltpu.VMEM((RANK, RANK), f32),
            pltpu.VMEM((PLANE, PIECE, RANK), f32),
            pltpu.VMEM((PLANE, PIECE, RANK), f32),
            pltpu.VMEM((PIECE, RANK), f32),
            pltpu.VMEM((PLANES, PIECE, RANK), f32),
            pltpu.VMEM((PIECE, RANK), f32),
            pltpu.VMEM((PLANE, PIECE, RANK), f32),
            pltpu.VMEM((STEPS, UNIT, RANK), f32),
            pltpu.VMEM((STEPS, UNIT, RANK), f32),
            pltpu.VMEM((STEPS, UNIT, RANK), f32),
            pltpu.VMEM((STEPS, UNIT, RANK), f32),
            dma((CHUNKS,)), dma((CHUNKS,)), dma((CHUNKS,)), dma, dma, dma, dma((2,)), dma((2,)), dma((2,)),
            dma((STEPS, parts)), dma((STEPS, parts)), dma((STEPS, parts)), dma((STEPS, parts)),
        ],
        compiler_params=pltpu.CompilerParams(
            collective_id=0, has_side_effects=True, vmem_limit_bytes=48 * 1024 * 1024
        ),
    )(slot_items, user_rows, conf, user_factors, prev_factors)


def solution(mesh):
    in_specs = (
        P(("grp", "own"), None),
        P(("grp", "own")),
        P(("grp", "own")),
        P(("grp", "own")),
        P(),
        P("own", "grp", None),
    )
    out_specs = P("own", "grp", None)
    return jax.shard_map(
        on_device, mesh=mesh, in_specs=in_specs, out_specs=out_specs, check_vma=False
    )
```

```python
import jax
import jax.numpy as jnp
from jax import lax
from jax.experimental import pallas as pl
from jax.experimental.pallas import tpu as pltpu
from jax.sharding import PartitionSpec as P

CG_STEPS = 3
RIDGE = 4.0
EPSILON = 1e-06

RANK = 128
DEPTH = 6
USERS = 4096
WINDOW = 1024
SIDE = 4
PLANES = 32
PLANE = 32
PEERS = 2 * PLANE
ITEMS = WINDOW // PEERS
STEPS = ITEMS // 2
PADDED = 8
LENGTH = PEERS * PADDED
CHUNKS = ((0, 1), (1, 3), (4, 4))
SIZES = tuple(2 * steps * PADDED for _, steps in CHUNKS)
UNIT = RANK + 8
CUTS = ((0, 64), (64, 72))
PIECE = RANK // PLANE
MESH = pl.DeviceIdType.MESH


def place():
    grp = lax.axis_index("grp")
    own = lax.axis_index("own")
    return grp // SIDE, grp % SIDE, own // 2, own % 2


def wrapped(number, size):
    number = jnp.where(number < 0, number + size, number)
    return jnp.where(number >= size, number - size, number)


def other_plane(z, core):
    away = 1 - 2 * (z % 2)
    return wrapped(z + away * (1 - 2 * core), PLANES)


def along(step):
    _, _, z, core = place()
    return (lax.axis_index("grp"), wrapped(z + step, PLANES) * 2 + core)


def each_peer(act):
    gx, gy, _, core = place()
    cores = (core, 1 - core)
    columns = [wrapped(gy + step, SIDE) for step in range(SIDE)]

    def ring(step, line):
        for dy in (2, 3, 1, 0):
            for dc in range(2):
                grp = line * SIDE + columns[dy]
                act(grp, cores[dc], cores[dc] * 16 + grp, step == 2 if dy + dc == 0 else None)
        return wrapped(line + 1, SIDE)

    lax.fori_loop(0, SIDE, ring, wrapped(gx + 2, SIDE))


def unless(first, act):
    if first is None:
        act()
    else:
        pl.when(jnp.logical_not(first))(act)


def solve(system, rhs, start):
    row = lax.broadcasted_iota(jnp.int32, (RANK, RANK), 0)
    col = lax.broadcasted_iota(jnp.int32, (RANK, RANK), 1)
    same = row == col

    def applied_to(vector):
        column = jnp.sum(system * vector, axis=1, keepdims=True)
        return jnp.sum(jnp.where(same, column, 0.0), axis=0, keepdims=True)

    answer = start
    residual = rhs - applied_to(start)
    direction = residual
    norm_now = jnp.sum(residual * residual, axis=1, keepdims=True)
    for step in range(CG_STEPS):
        applied = applied_to(direction)
        step_size = norm_now / (jnp.sum(direction * applied, axis=1, keepdims=True) + EPSILON)
        answer = answer + step_size * direction
        residual = residual - step_size * applied
        norm_next = jnp.sum(residual * residual, axis=1, keepdims=True)
        direction = residual + (norm_next / (norm_now + EPSILON)) * direction
        norm_now = norm_next
    return answer


def kernel(
    items, rows, conf, users, start, out,
    wide, stage, send, recv, flat, conf_wide, conf_parts, conf_all, weight_all,
    gram_own, gram_cut, gram_parts, gram_piece, gram_all, piece_send, piece_recv,
    up_send, up_recv, down_send, down_recv,
    send_sem, recv_sem, self_sem, part_sem, all_sem, piece_send_sem, piece_recv_sem,
    up_send_sem, up_recv_sem, down_send_sem, down_recv_sem,
):
    _, _, z, core = place()
    me = core * 16 + lax.axis_index("grp")
    barrier = pltpu.get_barrier_semaphore()

    def greet(device):
        pl.semaphore_signal(barrier, inc=1, device_id=device, device_id_type=MESH)

    far_plane = other_plane(z, core)
    far_planes = (other_plane(z, 0), other_plane(z, 1))

    def greet_plane(grp, pc, _, first):
        unless(first, lambda: greet((grp, z * 2 + pc)))
        greet((grp, far_plane * 2 + pc))

    each_peer(greet_plane)
    for away in (2, -2, 4, -4):
        greet(along(away))

    def widen_users(block, carry):
        at = pl.ds(pl.multiple_of(block * 512, 512), 512)
        wide[at, :] = users[at, :].astype(jnp.float32)
        return carry

    lax.fori_loop(0, USERS // 512, widen_users, 0)

    def item_of(base, d, index):
        step = index // 2
        away = STEPS - step if index % 2 == 0 else step - (STEPS - 1)
        return items[wrapped(base + 2 * away, PLANES) * PLANE + d]

    def each_receiver(act):
        for far in range(2):
            for pc in range(2):
                base = far_planes[pc] if far else z

                def one(grp, carry):
                    act(far * PLANE + pc * 16 + grp, pc * 16 + grp, base)
                    return carry

                lax.fori_loop(0, 16, one, 0)

    def spread_conf():
        spread_row = lax.broadcasted_iota(jnp.int32, (8, RANK), 0)
        spread_col = lax.broadcasted_iota(jnp.int32, (8, RANK), 1)
        mine = spread_col // PADDED == me % 16
        spread = jnp.where(jnp.logical_and(mine, spread_col % PADDED == spread_row), 1.0, 0.0).astype(jnp.bfloat16)
        conf_wide[...] = jnp.dot(conf[...], spread, preferred_element_type=jnp.float32)

    def gather(chunk):
        first, count = CHUNKS[chunk]
        group, size = 2 * count, SIZES[chunk]

        def owner(to, d, base):
            for index in range(group):
                item = item_of(base, d, 2 * first + index)
                for slot in range(DEPTH):
                    row = rows[item * DEPTH + slot]
                    stage[pl.ds(to * size + slot * group + index, 1), :] = wide[pl.ds(row, 1), :]
                stage[pl.ds(to * size + DEPTH * group + index, 1), :] = conf_wide[pl.ds(item, 1), :]

        each_receiver(owner)

        def narrow(block, carry):
            at = pl.ds(pl.multiple_of(block * size * 4, size * 4), size * 4)
            part = stage[at, :].astype(jnp.bfloat16)
            send[chunk, pl.ds(block * 4, 4), pl.ds(0, size)] = part.reshape(4, size, RANK)
            return carry

        lax.fori_loop(0, PEERS // 4, narrow, 0)

    def post_rows(chunk):
        size = pl.ds(0, SIZES[chunk])

        def one(grp, pc, d, first):
            def near():
                pltpu.make_async_remote_copy(
                    src_ref=send.at[chunk, d, size], dst_ref=recv.at[chunk, me, size], send_sem=send_sem.at[chunk],
                    recv_sem=recv_sem.at[chunk], device_id=(grp, z * 2 + pc), device_id_type=MESH,
                ).start()

            unless(first, near)
            far = jnp.where(pc == 0, far_planes[0], far_planes[1])
            pltpu.make_async_remote_copy(
                src_ref=send.at[chunk, PLANE + d, size], dst_ref=recv.at[chunk, PLANE + me, size],
                send_sem=send_sem.at[chunk], recv_sem=recv_sem.at[chunk], device_id=(grp, far * 2 + pc),
                device_id_type=MESH,
            ).start()

        each_peer(one)
        own_rows(chunk).start()

    def own_rows(chunk):
        size = pl.ds(0, SIZES[chunk])
        return pltpu.make_async_copy(send.at[chunk, me, size], recv.at[chunk, me, size], self_sem.at[chunk])

    def wait_rows(ref, chunk, sem):
        part = ref.at[chunk, pl.ds(0, PEERS - 1), pl.ds(0, SIZES[chunk])]
        pltpu.make_async_copy(part, part, sem.at[chunk]).wait()

    def wait_blocks(ref, count, sem):
        pltpu.make_async_copy(ref.at[pl.ds(0, count)], ref.at[pl.ds(0, count)], sem).wait()

    def take_rows(chunk):
        wait_rows(recv, chunk, recv_sem)
        own_rows(chunk).wait()
        group, size = 2 * CHUNKS[chunk][1], SIZES[chunk]
        used = DEPTH * group
        tail = used // 8 * 8
        live = lax.broadcasted_iota(jnp.int32, (size, RANK), 0) < used

        def sixteen(part, carry):
            def widen(index, total):
                source = part * 16 + index
                block = recv[chunk, source, pl.ds(0, size)].astype(jnp.float32)
                flat[pl.ds(pl.multiple_of(source * size, size), size), :] = jnp.where(live, block, 0.0)
                return total + block[tail:]

            total = lax.fori_loop(0, 16, widen, jnp.zeros((size - tail, RANK), jnp.float32))
            conf_parts[part, pl.ds(0, size - tail)] = total
            return carry

        lax.fori_loop(0, PEERS // 16, sixteen, 0)
        for part in range(PEERS // 16):
            at = pl.ds(part * RANK, RANK)
            conf_all[chunk, pl.ds(0, group), at] = conf_parts[part, pl.ds(used - tail, group)]
        values = conf_all[chunk]
        weight = (1.0 + values).astype(jnp.bfloat16).astype(jnp.float32)
        weight_all[chunk] = jnp.where(values > 0.0, weight, 0.0)

    def own_gram():
        gram_own[...] = jnp.zeros_like(gram_own)

        def one_block(block, carry):
            part = users[pl.ds(pl.multiple_of(block * 512, 512), 512), :]
            gram_own[...] += lax.dot_general(part, part, (((0,), (0,)), ((), ())), preferred_element_type=jnp.float32)
            return carry

        lax.fori_loop(0, USERS // 512, one_block, 0)
        for index in range(PLANE):
            gram_cut[index] = gram_own[pl.ds(index * PIECE, PIECE), :]

    def post_gram():
        def one(grp, pc, d, first):
            def start_copy():
                pltpu.make_async_remote_copy(
                    src_ref=gram_cut.at[d], dst_ref=gram_parts.at[me], send_sem=part_sem.at[0],
                    recv_sem=part_sem.at[1], device_id=(grp, z * 2 + pc), device_id_type=MESH,
                ).start()

            unless(first, start_copy)

        each_peer(one)
        gram_parts[me] = gram_cut[me]

    def pair_copy():
        return pltpu.make_async_remote_copy(
            src_ref=piece_send.at[0], dst_ref=piece_recv.at[0], send_sem=piece_send_sem.at[0],
            recv_sem=piece_recv_sem.at[0], device_id=(lax.axis_index("grp"), far_plane * 2 + core), device_id_type=MESH,
        )

    def next_copy():
        return pltpu.make_async_remote_copy(
            src_ref=piece_send.at[1], dst_ref=piece_recv.at[1], send_sem=piece_send_sem.at[1],
            recv_sem=piece_recv_sem.at[1], device_id=along(2), device_id_type=MESH,
        )

    def round_copy(turn, down):
        at = 2 + 4 * down + turn
        return pltpu.make_async_remote_copy(
            src_ref=piece_send.at[2] if turn == 0 else piece_recv.at[at - 1], dst_ref=piece_recv.at[at],
            send_sem=piece_send_sem.at[at], recv_sem=piece_recv_sem.at[at], device_id=along(-4 if down else 4),
            device_id_type=MESH,
        )

    def pair_turn():
        wait_blocks(gram_parts, PLANE - 1, part_sem.at[1])
        piece_send[0] = jnp.sum(gram_parts[...], axis=0)
        pair_copy().start()

    def next_turn():
        pair_copy().wait_recv()
        piece_send[1] = piece_send[0] + piece_recv[0]
        next_copy().start()

    def round_turn(turn):
        if turn == 0:
            next_copy().wait_recv()
            piece_send[2] = piece_send[1] + piece_recv[1]
        else:
            round_copy(turn - 1, 0).wait_recv()
            if turn < 4:
                round_copy(turn - 1, 1).wait_recv()
        if turn < 4:
            round_copy(turn, 0).start()
        if turn < 3:
            round_copy(turn, 1).start()

    def post_total():
        total = jnp.sum(piece_recv[pl.ds(2, 7)], axis=0) + piece_send[2]
        gram_piece[...] = total

        def one(grp, pc, d, first):
            def start_copy():
                pltpu.make_async_remote_copy(
                    src_ref=gram_piece, dst_ref=gram_all.at[me], send_sem=all_sem.at[0],
                    recv_sem=all_sem.at[1], device_id=(grp, z * 2 + pc), device_id_type=MESH,
                ).start()

            unless(first, start_copy)

        each_peer(one)
        gram_all[me] = total

    def beside(step):
        if step == 0:
            next_turn()
        elif step < 6:
            round_turn(step - 1)
        if step == 5:
            post_total()

    def item_gram(into, chunk, index):
        values = flat[pl.ds(index, LENGTH, stride=2 * CHUNKS[chunk][1]), :]
        scaled = (jnp.transpose(values) * conf_all[chunk, pl.ds(index, 1), :]).astype(jnp.bfloat16)
        weights = jnp.broadcast_to(weight_all[chunk, pl.ds(index, 1), :], (16, LENGTH)).astype(jnp.bfloat16)
        left = jnp.concatenate([scaled, weights], axis=0)
        product = jnp.dot(left, values.astype(jnp.bfloat16), preferred_element_type=jnp.float32)
        into[...] = product[:UNIT]

    def up_copy(step, part):
        first, count = CUTS[part]
        at = pl.ds(first, count)
        return pltpu.make_async_remote_copy(
            src_ref=up_send.at[step, at], dst_ref=up_recv.at[step, at], send_sem=up_send_sem.at[step, part],
            recv_sem=up_recv_sem.at[step, part], device_id=along(2), device_id_type=MESH,
        )

    def down_copy(step, part):
        first, count = CUTS[part]
        at = pl.ds(first, count)
        return pltpu.make_async_remote_copy(
            src_ref=down_send.at[step, at], dst_ref=down_recv.at[step, at], send_sem=down_send_sem.at[step, part],
            recv_sem=down_recv_sem.at[step, part], device_id=along(-2), device_id_type=MESH,
        )

    stage[...] = jnp.zeros_like(stage)
    spread_conf()
    gather(0)
    pl.semaphore_wait(barrier, PLANE - 1 + PLANE + 4)
    post_rows(0)
    own_gram()
    post_gram()
    gather(1)
    post_rows(1)
    gather(2)
    post_rows(2)

    def chain(step, chunk):
        index = (step - CHUNKS[chunk][0]) * 2
        item_gram(up_send.at[step], chunk, index)
        item_gram(down_send.at[step], chunk, index + 1)
        for part, (begin, count) in enumerate(CUTS):
            at = pl.ds(begin, count)
            if step > 0:
                up_copy(step - 1, part).wait_recv()
                up_send[step, at] += up_recv[step - 1, at]
            up_copy(step, part).start()
            if step > 0:
                down_copy(step - 1, part).wait_recv()
                down_send[step, at] += down_recv[step - 1, at]
            if step < STEPS - 1:
                down_copy(step, part).start()
        beside(step)

    for chunk, (first, count) in enumerate(CHUNKS):
        if chunk == 0:
            pair_turn()
        take_rows(chunk)
        for step in range(first, first + count):
            chain(step, chunk)
    row = lax.broadcasted_iota(jnp.int32, (RANK, RANK), 0)
    col = lax.broadcasted_iota(jnp.int32, (RANK, RANK), 1)
    wait_blocks(gram_all, PLANE - 1, all_sem.at[1])
    for index in range(PLANE):
        gram_own[pl.ds(index * PIECE, PIECE), :] = gram_all[index]
    gram_own[...] += down_send[STEPS - 1, pl.ds(0, RANK)] + jnp.where(row == col, RIDGE, 0.0)
    for part in range(len(CUTS)):
        up_copy(STEPS - 1, part).wait_recv()
    system = gram_own[...] + up_recv[STEPS - 1, pl.ds(0, RANK)]
    rhs = down_send[STEPS - 1, pl.ds(RANK, 1)] + up_recv[STEPS - 1, pl.ds(RANK, 1)]
    out[0] = solve(system, rhs, start[0])

    for chunk in range(len(CHUNKS)):
        wait_rows(send, chunk, send_sem)
    wait_blocks(gram_parts, PLANE - 1, part_sem.at[0])
    pair_copy().wait_send()
    next_copy().wait_send()
    for turn in range(4):
        round_copy(turn, 0).wait_send()
    for turn in range(3):
        round_copy(turn, 1).wait_send()
    wait_blocks(gram_all, PLANE - 1, all_sem.at[0])

    def drain(step, carry):
        for part in range(len(CUTS)):
            up_copy(step, part).wait_send()

            @pl.when(step < STEPS - 1)
            def _():
                down_copy(step, part).wait_send()

        return carry

    lax.fori_loop(0, STEPS, drain, 0)


def on_device(user_factors, user_rows, row_counts, confidence, slot_items, prev_factors):
    conf = confidence.reshape(WINDOW, DEPTH)
    live = lax.broadcasted_iota(jnp.int32, (WINDOW, DEPTH), 1) < row_counts[:, None]
    conf = jnp.pad(jnp.where(live, conf, jnp.zeros_like(conf)), ((0, 0), (0, 8 - DEPTH)))
    vmem = pl.BlockSpec(memory_space=pltpu.VMEM)
    smem = pl.BlockSpec(memory_space=pltpu.SMEM)
    f32, bf16 = jnp.float32, jnp.bfloat16
    dma = pltpu.SemaphoreType.DMA
    parts, chunks = len(CUTS), len(CHUNKS)
    return pl.pallas_call(
        kernel,
        out_shape=jax.ShapeDtypeStruct((1, 1, RANK), f32),
        in_specs=[smem, smem, vmem, vmem, vmem],
        out_specs=vmem,
        scratch_shapes=[
            pltpu.VMEM((USERS, RANK), f32),
            pltpu.VMEM((PEERS * max(SIZES), RANK), f32),
            pltpu.VMEM((len(CHUNKS), PEERS, max(SIZES), RANK), bf16),
            pltpu.VMEM((len(CHUNKS), PEERS, max(SIZES), RANK), bf16),
            pltpu.VMEM((PEERS * max(SIZES), RANK), f32),
            pltpu.VMEM((WINDOW, RANK), f32),
            pltpu.VMEM((PEERS // 16, 16, RANK), f32),
            pltpu.VMEM((len(CHUNKS), 8, LENGTH), f32),
            pltpu.VMEM((len(CHUNKS), 8, LENGTH), f32),
            pltpu.VMEM((RANK, RANK), f32),
            pltpu.VMEM((PLANE, PIECE, RANK), f32),
            pltpu.VMEM((PLANE, PIECE, RANK), f32),
            pltpu.VMEM((PIECE, RANK), f32),
            pltpu.VMEM((PLANE, PIECE, RANK), f32),
            pltpu.VMEM((3, PIECE, RANK), f32),
            pltpu.VMEM((9, PIECE, RANK), f32),
            pltpu.VMEM((STEPS, UNIT, RANK), f32),
            pltpu.VMEM((STEPS, UNIT, RANK), f32),
            pltpu.VMEM((STEPS, UNIT, RANK), f32),
            pltpu.VMEM((STEPS, UNIT, RANK), f32),
            dma((chunks,)), dma((chunks,)), dma((chunks,)), dma((2,)), dma((2,)), dma((9,)), dma((9,)),
            dma((STEPS, parts)), dma((STEPS, parts)), dma((STEPS, parts)), dma((STEPS, parts)),
        ],
        compiler_params=pltpu.CompilerParams(
            collective_id=0, has_side_effects=True, vmem_limit_bytes=48 * 1024 * 1024
        ),
    )(slot_items, user_rows, conf, user_factors, prev_factors)


def solution(mesh):
    in_specs = (
        P(("grp", "own"), None),
        P(("grp", "own")),
        P(("grp", "own")),
        P(("grp", "own")),
        P(),
        P("own", "grp", None),
    )
    out_specs = P("own", "grp", None)
    return jax.shard_map(
        on_device, mesh=mesh, in_specs=in_specs, out_specs=out_specs, check_vma=False
    )
```

```python
import jax
import jax.numpy as jnp
from jax import lax
from jax.experimental import pallas as pl
from jax.experimental.pallas import tpu as pltpu
from jax.sharding import PartitionSpec as P

CG_STEPS = 3
RIDGE = 4.0
EPSILON = 1e-06

RANK = 128
DEPTH = 6
USERS = 4096
WINDOW = 1024
SIDE = 4
PLANES = 32
PLANE = 32
PEERS = 2 * PLANE
ITEMS = WINDOW // PEERS
STEPS = ITEMS // 2
PADDED = 8
LENGTH = PEERS * PADDED
CHUNKS = ((0, 1), (1, 1), (2, 1), (3, 1), (4, 2), (6, 2))
AHEAD = 2
SIZES = tuple(2 * steps * PADDED for _, steps in CHUNKS)
UNIT = RANK + 8
CUTS = ((0, 64), (64, 72))
PIECE = RANK // PLANE
MESH = pl.DeviceIdType.MESH


def place():
    grp = lax.axis_index("grp")
    own = lax.axis_index("own")
    return grp // SIDE, grp % SIDE, own // 2, own % 2


def wrapped(number, size):
    number = jnp.where(number < 0, number + size, number)
    return jnp.where(number >= size, number - size, number)


def other_plane(z, core):
    away = 1 - 2 * (z % 2)
    return wrapped(z + away * (1 - 2 * core), PLANES)


def along(step):
    _, _, z, core = place()
    return (lax.axis_index("grp"), wrapped(z + step, PLANES) * 2 + core)


def each_peer(act):
    gx, gy, _, core = place()
    cores = (core, 1 - core)
    columns = [wrapped(gy + step, SIDE) for step in range(SIDE)]

    def ring(step, line):
        for dy in (2, 3, 1, 0):
            for dc in range(2):
                grp = line * SIDE + columns[dy]
                act(grp, cores[dc], cores[dc] * 16 + grp, step == 2 if dy + dc == 0 else None)
        return wrapped(line + 1, SIDE)

    lax.fori_loop(0, SIDE, ring, wrapped(gx + 2, SIDE))


def unless(first, act):
    if first is None:
        act()
    else:
        pl.when(jnp.logical_not(first))(act)


def solve(system, rhs, start):
    row = lax.broadcasted_iota(jnp.int32, (RANK, RANK), 0)
    col = lax.broadcasted_iota(jnp.int32, (RANK, RANK), 1)
    same = row == col

    def applied_to(vector):
        column = jnp.sum(system * vector, axis=1, keepdims=True)
        return jnp.sum(jnp.where(same, column, 0.0), axis=0, keepdims=True)

    answer = start
    residual = rhs - applied_to(start)
    direction = residual
    norm_now = jnp.sum(residual * residual, axis=1, keepdims=True)
    for step in range(CG_STEPS):
        applied = applied_to(direction)
        step_size = norm_now / (jnp.sum(direction * applied, axis=1, keepdims=True) + EPSILON)
        answer = answer + step_size * direction
        residual = residual - step_size * applied
        norm_next = jnp.sum(residual * residual, axis=1, keepdims=True)
        direction = residual + (norm_next / (norm_now + EPSILON)) * direction
        norm_now = norm_next
    return answer


def kernel(
    items, rows, conf, users, start, out,
    wide, stage, send, recv, flat, conf_wide, conf_parts, conf_all, weight_all,
    gram_own, gram_cut, gram_parts, gram_piece, gram_all, piece_send, piece_recv,
    up_send, up_recv, down_send, down_recv,
    send_sem, recv_sem, self_sem, part_sem, all_sem, piece_send_sem, piece_recv_sem,
    up_send_sem, up_recv_sem, down_send_sem, down_recv_sem,
):
    _, _, z, core = place()
    me = core * 16 + lax.axis_index("grp")
    barrier = pltpu.get_barrier_semaphore()

    def greet(device):
        pl.semaphore_signal(barrier, inc=1, device_id=device, device_id_type=MESH)

    far_plane = other_plane(z, core)
    far_planes = (other_plane(z, 0), other_plane(z, 1))

    def greet_plane(grp, pc, _, first):
        unless(first, lambda: greet((grp, z * 2 + pc)))
        greet((grp, far_plane * 2 + pc))

    each_peer(greet_plane)
    for away in (2, -2, 4, -4):
        greet(along(away))

    def widen_users(block, carry):
        at = pl.ds(pl.multiple_of(block * 512, 512), 512)
        wide[at, :] = users[at, :].astype(jnp.float32)
        return carry

    lax.fori_loop(0, USERS // 512, widen_users, 0)

    def item_of(base, d, index):
        step = index // 2
        away = STEPS - step if index % 2 == 0 else step - (STEPS - 1)
        return items[wrapped(base + 2 * away, PLANES) * PLANE + d]

    def each_receiver(act):
        for far in range(2):
            for pc in range(2):
                base = far_planes[pc] if far else z

                def one(grp, carry):
                    act(far * PLANE + pc * 16 + grp, pc * 16 + grp, base)
                    return carry

                lax.fori_loop(0, 16, one, 0)

    def spread_conf():
        spread_row = lax.broadcasted_iota(jnp.int32, (8, RANK), 0)
        spread_col = lax.broadcasted_iota(jnp.int32, (8, RANK), 1)
        mine = spread_col // PADDED == me % 16
        spread = jnp.where(jnp.logical_and(mine, spread_col % PADDED == spread_row), 1.0, 0.0).astype(jnp.bfloat16)
        conf_wide[...] = jnp.dot(conf[...], spread, preferred_element_type=jnp.float32)

    def gather(chunk):
        first, count = CHUNKS[chunk]
        group, size = 2 * count, SIZES[chunk]

        def owner(to, d, base):
            for index in range(group):
                item = item_of(base, d, 2 * first + index)
                for slot in range(DEPTH):
                    row = rows[item * DEPTH + slot]
                    stage[pl.ds(to * size + slot * group + index, 1), :] = wide[pl.ds(row, 1), :]
                stage[pl.ds(to * size + DEPTH * group + index, 1), :] = conf_wide[pl.ds(item, 1), :]

        each_receiver(owner)

        def narrow(block, carry):
            at = pl.ds(pl.multiple_of(block * size * 4, size * 4), size * 4)
            part = stage[at, :].astype(jnp.bfloat16)
            send[chunk, pl.ds(block * 4, 4), pl.ds(0, size)] = part.reshape(4, size, RANK)
            return carry

        lax.fori_loop(0, PEERS // 4, narrow, 0)

    def post_rows(chunk):
        size = pl.ds(0, SIZES[chunk])

        def one(grp, pc, d, first):
            def near():
                pltpu.make_async_remote_copy(
                    src_ref=send.at[chunk, d, size], dst_ref=recv.at[chunk, me, size], send_sem=send_sem.at[chunk],
                    recv_sem=recv_sem.at[chunk], device_id=(grp, z * 2 + pc), device_id_type=MESH,
                ).start()

            unless(first, near)
            far = jnp.where(pc == 0, far_planes[0], far_planes[1])
            pltpu.make_async_remote_copy(
                src_ref=send.at[chunk, PLANE + d, size], dst_ref=recv.at[chunk, PLANE + me, size],
                send_sem=send_sem.at[chunk], recv_sem=recv_sem.at[chunk], device_id=(grp, far * 2 + pc),
                device_id_type=MESH,
            ).start()

        each_peer(one)
        own_rows(chunk).start()

    def own_rows(chunk):
        size = pl.ds(0, SIZES[chunk])
        return pltpu.make_async_copy(send.at[chunk, me, size], recv.at[chunk, me, size], self_sem.at[chunk])

    def wait_rows(ref, chunk, sem):
        part = ref.at[chunk, pl.ds(0, PEERS - 1), pl.ds(0, SIZES[chunk])]
        pltpu.make_async_copy(part, part, sem.at[chunk]).wait()

    def wait_blocks(ref, count, sem):
        pltpu.make_async_copy(ref.at[pl.ds(0, count)], ref.at[pl.ds(0, count)], sem).wait()

    def take_rows(chunk):
        wait_rows(recv, chunk, recv_sem)
        own_rows(chunk).wait()
        group, size = 2 * CHUNKS[chunk][1], SIZES[chunk]
        used = DEPTH * group
        tail = used // 8 * 8
        live = lax.broadcasted_iota(jnp.int32, (size, RANK), 0) < used

        def sixteen(part, carry):
            def widen(index, total):
                source = part * 16 + index
                block = recv[chunk, source, pl.ds(0, size)].astype(jnp.float32)
                flat[pl.ds(pl.multiple_of(source * size, size), size), :] = jnp.where(live, block, 0.0)
                return total + block[tail:]

            total = lax.fori_loop(0, 16, widen, jnp.zeros((size - tail, RANK), jnp.float32))
            conf_parts[part, pl.ds(0, size - tail)] = total
            return carry

        lax.fori_loop(0, PEERS // 16, sixteen, 0)
        for part in range(PEERS // 16):
            at = pl.ds(part * RANK, RANK)
            conf_all[chunk, pl.ds(0, group), at] = conf_parts[part, pl.ds(used - tail, group)]
        values = conf_all[chunk]
        weight = (1.0 + values).astype(jnp.bfloat16).astype(jnp.float32)
        weight_all[chunk] = jnp.where(values > 0.0, weight, 0.0)

    def own_gram():
        gram_own[...] = jnp.zeros_like(gram_own)

        def one_block(block, carry):
            part = users[pl.ds(pl.multiple_of(block * 512, 512), 512), :]
            gram_own[...] += lax.dot_general(part, part, (((0,), (0,)), ((), ())), preferred_element_type=jnp.float32)
            return carry

        lax.fori_loop(0, USERS // 512, one_block, 0)
        for index in range(PLANE):
            gram_cut[index] = gram_own[pl.ds(index * PIECE, PIECE), :]

    def post_gram():
        def one(grp, pc, d, first):
            def start_copy():
                pltpu.make_async_remote_copy(
                    src_ref=gram_cut.at[d], dst_ref=gram_parts.at[me], send_sem=part_sem.at[0],
                    recv_sem=part_sem.at[1], device_id=(grp, z * 2 + pc), device_id_type=MESH,
                ).start()

            unless(first, start_copy)

        each_peer(one)
        gram_parts[me] = gram_cut[me]

    def pair_copy():
        return pltpu.make_async_remote_copy(
            src_ref=piece_send.at[0], dst_ref=piece_recv.at[0], send_sem=piece_send_sem.at[0],
            recv_sem=piece_recv_sem.at[0], device_id=(lax.axis_index("grp"), far_plane * 2 + core), device_id_type=MESH,
        )

    def next_copy():
        return pltpu.make_async_remote_copy(
            src_ref=piece_send.at[1], dst_ref=piece_recv.at[1], send_sem=piece_send_sem.at[1],
            recv_sem=piece_recv_sem.at[1], device_id=along(2), device_id_type=MESH,
        )

    def round_copy(turn, down):
        at = 2 + 4 * down + turn
        return pltpu.make_async_remote_copy(
            src_ref=piece_send.at[2] if turn == 0 else piece_recv.at[at - 1], dst_ref=piece_recv.at[at],
            send_sem=piece_send_sem.at[at], recv_sem=piece_recv_sem.at[at], device_id=along(-4 if down else 4),
            device_id_type=MESH,
        )

    def pair_turn():
        wait_blocks(gram_parts, PLANE - 1, part_sem.at[1])
        piece_send[0] = jnp.sum(gram_parts[...], axis=0)
        pair_copy().start()

    def next_turn():
        pair_copy().wait_recv()
        piece_send[1] = piece_send[0] + piece_recv[0]
        next_copy().start()

    def round_turn(turn):
        if turn == 0:
            next_copy().wait_recv()
            piece_send[2] = piece_send[1] + piece_recv[1]
        else:
            round_copy(turn - 1, 0).wait_recv()
            if turn < 4:
                round_copy(turn - 1, 1).wait_recv()
        if turn < 4:
            round_copy(turn, 0).start()
        if turn < 3:
            round_copy(turn, 1).start()

    def post_total():
        total = jnp.sum(piece_recv[pl.ds(2, 7)], axis=0) + piece_send[2]
        gram_piece[...] = total

        def one(grp, pc, d, first):
            def start_copy():
                pltpu.make_async_remote_copy(
                    src_ref=gram_piece, dst_ref=gram_all.at[me], send_sem=all_sem.at[0],
                    recv_sem=all_sem.at[1], device_id=(grp, z * 2 + pc), device_id_type=MESH,
                ).start()

            unless(first, start_copy)

        each_peer(one)
        gram_all[me] = total

    def beside(step):
        if step == 0:
            next_turn()
        elif step < 6:
            round_turn(step - 1)
        if step == 5:
            post_total()

    def item_gram(into, chunk, index):
        values = flat[pl.ds(index, LENGTH, stride=2 * CHUNKS[chunk][1]), :]
        scaled = (jnp.transpose(values) * conf_all[chunk, pl.ds(index, 1), :]).astype(jnp.bfloat16)
        weights = jnp.broadcast_to(weight_all[chunk, pl.ds(index, 1), :], (16, LENGTH)).astype(jnp.bfloat16)
        left = jnp.concatenate([scaled, weights], axis=0)
        product = jnp.dot(left, values.astype(jnp.bfloat16), preferred_element_type=jnp.float32)
        into[...] = product[:UNIT]

    def up_copy(step, part):
        first, count = CUTS[part]
        at = pl.ds(first, count)
        return pltpu.make_async_remote_copy(
            src_ref=up_send.at[step, at], dst_ref=up_recv.at[step, at], send_sem=up_send_sem.at[step, part],
            recv_sem=up_recv_sem.at[step, part], device_id=along(2), device_id_type=MESH,
        )

    def down_copy(step, part):
        first, count = CUTS[part]
        at = pl.ds(first, count)
        return pltpu.make_async_remote_copy(
            src_ref=down_send.at[step, at], dst_ref=down_recv.at[step, at], send_sem=down_send_sem.at[step, part],
            recv_sem=down_recv_sem.at[step, part], device_id=along(-2), device_id_type=MESH,
        )

    stage[...] = jnp.zeros_like(stage)
    spread_conf()
    gather(0)
    pl.semaphore_wait(barrier, PLANE - 1 + PLANE + 4)
    post_rows(0)
    own_gram()
    post_gram()
    for chunk in range(1, AHEAD):
        gather(chunk)
        post_rows(chunk)

    def chain(step, chunk):
        index = (step - CHUNKS[chunk][0]) * 2
        item_gram(up_send.at[step], chunk, index)
        item_gram(down_send.at[step], chunk, index + 1)
        for part, (begin, count) in enumerate(CUTS):
            at = pl.ds(begin, count)
            if step > 0:
                up_copy(step - 1, part).wait_recv()
                up_send[step, at] += up_recv[step - 1, at]
            up_copy(step, part).start()
            if step > 0:
                down_copy(step - 1, part).wait_recv()
                down_send[step, at] += down_recv[step - 1, at]
            if step < STEPS - 1:
                down_copy(step, part).start()
        if AHEAD + step < len(CHUNKS):
            gather(AHEAD + step)
            post_rows(AHEAD + step)
        beside(step)

    for chunk, (first, count) in enumerate(CHUNKS):
        if chunk == 0:
            pair_turn()
        take_rows(chunk)
        for step in range(first, first + count):
            chain(step, chunk)
    row = lax.broadcasted_iota(jnp.int32, (RANK, RANK), 0)
    col = lax.broadcasted_iota(jnp.int32, (RANK, RANK), 1)
    wait_blocks(gram_all, PLANE - 1, all_sem.at[1])
    for index in range(PLANE):
        gram_own[pl.ds(index * PIECE, PIECE), :] = gram_all[index]
    gram_own[...] += down_send[STEPS - 1, pl.ds(0, RANK)] + jnp.where(row == col, RIDGE, 0.0)
    for part in range(len(CUTS)):
        up_copy(STEPS - 1, part).wait_recv()
    system = gram_own[...] + up_recv[STEPS - 1, pl.ds(0, RANK)]
    rhs = down_send[STEPS - 1, pl.ds(RANK, 1)] + up_recv[STEPS - 1, pl.ds(RANK, 1)]
    out[0] = solve(system, rhs, start[0])

    for chunk in range(len(CHUNKS)):
        wait_rows(send, chunk, send_sem)
    wait_blocks(gram_parts, PLANE - 1, part_sem.at[0])
    pair_copy().wait_send()
    next_copy().wait_send()
    for turn in range(4):
        round_copy(turn, 0).wait_send()
    for turn in range(3):
        round_copy(turn, 1).wait_send()
    wait_blocks(gram_all, PLANE - 1, all_sem.at[0])

    def drain(step, carry):
        for part in range(len(CUTS)):
            up_copy(step, part).wait_send()

            @pl.when(step < STEPS - 1)
            def _():
                down_copy(step, part).wait_send()

        return carry

    lax.fori_loop(0, STEPS, drain, 0)


def on_device(user_factors, user_rows, row_counts, confidence, slot_items, prev_factors):
    conf = confidence.reshape(WINDOW, DEPTH)
    live = lax.broadcasted_iota(jnp.int32, (WINDOW, DEPTH), 1) < row_counts[:, None]
    conf = jnp.pad(jnp.where(live, conf, jnp.zeros_like(conf)), ((0, 0), (0, 8 - DEPTH)))
    vmem = pl.BlockSpec(memory_space=pltpu.VMEM)
    smem = pl.BlockSpec(memory_space=pltpu.SMEM)
    f32, bf16 = jnp.float32, jnp.bfloat16
    dma = pltpu.SemaphoreType.DMA
    parts, chunks = len(CUTS), len(CHUNKS)
    return pl.pallas_call(
        kernel,
        out_shape=jax.ShapeDtypeStruct((1, 1, RANK), f32),
        in_specs=[smem, smem, vmem, vmem, vmem],
        out_specs=vmem,
        scratch_shapes=[
            pltpu.VMEM((USERS, RANK), f32),
            pltpu.VMEM((PEERS * max(SIZES), RANK), f32),
            pltpu.VMEM((len(CHUNKS), PEERS, max(SIZES), RANK), bf16),
            pltpu.VMEM((len(CHUNKS), PEERS, max(SIZES), RANK), bf16),
            pltpu.VMEM((PEERS * max(SIZES), RANK), f32),
            pltpu.VMEM((WINDOW, RANK), f32),
            pltpu.VMEM((PEERS // 16, 16, RANK), f32),
            pltpu.VMEM((len(CHUNKS), 8, LENGTH), f32),
            pltpu.VMEM((len(CHUNKS), 8, LENGTH), f32),
            pltpu.VMEM((RANK, RANK), f32),
            pltpu.VMEM((PLANE, PIECE, RANK), f32),
            pltpu.VMEM((PLANE, PIECE, RANK), f32),
            pltpu.VMEM((PIECE, RANK), f32),
            pltpu.VMEM((PLANE, PIECE, RANK), f32),
            pltpu.VMEM((3, PIECE, RANK), f32),
            pltpu.VMEM((9, PIECE, RANK), f32),
            pltpu.VMEM((STEPS, UNIT, RANK), f32),
            pltpu.VMEM((STEPS, UNIT, RANK), f32),
            pltpu.VMEM((STEPS, UNIT, RANK), f32),
            pltpu.VMEM((STEPS, UNIT, RANK), f32),
            dma((chunks,)), dma((chunks,)), dma((chunks,)), dma((2,)), dma((2,)), dma((9,)), dma((9,)),
            dma((STEPS, parts)), dma((STEPS, parts)), dma((STEPS, parts)), dma((STEPS, parts)),
        ],
        compiler_params=pltpu.CompilerParams(
            collective_id=0, has_side_effects=True, vmem_limit_bytes=48 * 1024 * 1024
        ),
    )(slot_items, user_rows, conf, user_factors, prev_factors)


def solution(mesh):
    in_specs = (
        P(("grp", "own"), None),
        P(("grp", "own")),
        P(("grp", "own")),
        P(("grp", "own")),
        P(),
        P("own", "grp", None),
    )
    out_specs = P("own", "grp", None)
    return jax.shard_map(
        on_device, mesh=mesh, in_specs=in_specs, out_specs=out_specs, check_vma=False
    )
```

```python
import jax
import jax.numpy as jnp
from jax import lax
from jax.experimental import pallas as pl
from jax.experimental.pallas import tpu as pltpu
from jax.sharding import PartitionSpec as P

CG_STEPS = 3
RIDGE = 4.0
EPSILON = 1e-06

RANK = 128
DEPTH = 6
USERS = 4096
WINDOW = 1024
SIDE = 4
PLANES = 32
PLANE = 32
PEERS = 2 * PLANE
ITEMS = WINDOW // PEERS
STEPS = ITEMS // 2
PADDED = 8
LENGTH = PEERS * PADDED
CHUNKS = ((0, 1), (1, 1), (2, 1), (3, 1), (4, 2), (6, 2))
AHEAD = 2
SIZES = tuple(2 * steps * PADDED for _, steps in CHUNKS)
UNIT = RANK + 8
CUTS = ((0, 64), (64, 72))
PIECE = RANK // PLANE
MESH = pl.DeviceIdType.MESH


def place():
    grp = lax.axis_index("grp")
    own = lax.axis_index("own")
    return grp // SIDE, grp % SIDE, own // 2, own % 2


def wrapped(number, size):
    number = jnp.where(number < 0, number + size, number)
    return jnp.where(number >= size, number - size, number)


def other_plane(z, core):
    away = 1 - 2 * (z % 2)
    return wrapped(z + away * (1 - 2 * core), PLANES)


def along(step):
    _, _, z, core = place()
    return (lax.axis_index("grp"), wrapped(z + step, PLANES) * 2 + core)


def each_peer(act):
    gx, gy, _, core = place()
    cores = (core, 1 - core)
    columns = [wrapped(gy + step, SIDE) for step in range(SIDE)]

    def ring(step, line):
        for dy in (2, 3, 1, 0):
            for dc in range(2):
                grp = line * SIDE + columns[dy]
                act(grp, cores[dc], cores[dc] * 16 + grp, step == 2 if dy + dc == 0 else None)
        return wrapped(line + 1, SIDE)

    lax.fori_loop(0, SIDE, ring, wrapped(gx + 2, SIDE))


def unless(first, act):
    if first is None:
        act()
    else:
        pl.when(jnp.logical_not(first))(act)


def solve(system, rhs, start):
    row = lax.broadcasted_iota(jnp.int32, (RANK, RANK), 0)
    col = lax.broadcasted_iota(jnp.int32, (RANK, RANK), 1)
    same = row == col

    def applied_to(vector):
        column = jnp.sum(system * vector, axis=1, keepdims=True)
        return jnp.sum(jnp.where(same, column, 0.0), axis=0, keepdims=True)

    answer = start
    residual = rhs - applied_to(start)
    direction = residual
    norm_now = jnp.sum(residual * residual, axis=1, keepdims=True)
    for step in range(CG_STEPS):
        applied = applied_to(direction)
        step_size = norm_now / (jnp.sum(direction * applied, axis=1, keepdims=True) + EPSILON)
        answer = answer + step_size * direction
        residual = residual - step_size * applied
        norm_next = jnp.sum(residual * residual, axis=1, keepdims=True)
        direction = residual + (norm_next / (norm_now + EPSILON)) * direction
        norm_now = norm_next
    return answer


def kernel(
    items, rows, conf, users, start, out,
    wide, stage, send, recv, flat, conf_wide, conf_parts, conf_all, weight_all,
    gram_own, gram_cut, gram_parts, gram_piece, gram_all, piece_send, piece_recv,
    up_send, up_recv, down_send, down_recv,
    send_sem, recv_sem, self_sem, part_sem, all_sem, piece_send_sem, piece_recv_sem,
    up_send_sem, up_recv_sem, down_send_sem, down_recv_sem,
):
    _, _, z, core = place()
    me = core * 16 + lax.axis_index("grp")
    barrier = pltpu.get_barrier_semaphore()

    def greet(device):
        pl.semaphore_signal(barrier, inc=1, device_id=device, device_id_type=MESH)

    far_plane = other_plane(z, core)
    far_planes = (other_plane(z, 0), other_plane(z, 1))

    def greet_plane(grp, pc, _, first):
        unless(first, lambda: greet((grp, z * 2 + pc)))
        greet((grp, far_plane * 2 + pc))

    each_peer(greet_plane)
    for away in (2, -2, 4, -4):
        greet(along(away))

    def widen_users(block, carry):
        at = pl.ds(pl.multiple_of(block * 512, 512), 512)
        wide[at, :] = users[at, :].astype(jnp.float32)
        return carry

    lax.fori_loop(0, USERS // 512, widen_users, 0)

    def slots_of(base, index):
        step = index // 2
        away = STEPS - step if index % 2 == 0 else step - (STEPS - 1)
        return wrapped(base + 2 * away, PLANES) * PLANE

    def each_receiver(first, count, act):
        for far in range(2):
            for pc in range(2):
                base = far_planes[pc] if far else z
                begins = [slots_of(base, first + index) for index in range(count)]

                def two(pair, carry):
                    for grp in (2 * pair, 2 * pair + 1):
                        act(far * PLANE + pc * 16 + grp, pc * 16 + grp, begins)
                    return carry

                lax.fori_loop(0, 8, two, 0)

    def spread_conf():
        spread_row = lax.broadcasted_iota(jnp.int32, (8, RANK), 0)
        spread_col = lax.broadcasted_iota(jnp.int32, (8, RANK), 1)
        mine = spread_col // PADDED == me % 16
        spread = jnp.where(jnp.logical_and(mine, spread_col % PADDED == spread_row), 1.0, 0.0).astype(jnp.bfloat16)
        conf_wide[...] = jnp.dot(conf[...], spread, preferred_element_type=jnp.float32)

    def gather(chunk):
        first, count = CHUNKS[chunk]
        group, size = 2 * count, SIZES[chunk]

        def owner(to, d, begins):
            for index in range(group):
                item = items[begins[index] + d]
                for slot in range(DEPTH):
                    row = rows[item * DEPTH + slot]
                    stage[pl.ds(to * size + slot * group + index, 1), :] = wide[pl.ds(row, 1), :]
                stage[pl.ds(to * size + DEPTH * group + index, 1), :] = conf_wide[pl.ds(item, 1), :]

        each_receiver(2 * first, group, owner)

        def narrow(block, carry):
            at = pl.ds(pl.multiple_of(block * size * 4, size * 4), size * 4)
            part = stage[at, :].astype(jnp.bfloat16)
            send[chunk, pl.ds(block * 4, 4), pl.ds(0, size)] = part.reshape(4, size, RANK)
            return carry

        lax.fori_loop(0, PEERS // 4, narrow, 0)

    def post_rows(chunk):
        size = pl.ds(0, SIZES[chunk])

        def one(grp, pc, d, first):
            def near():
                pltpu.make_async_remote_copy(
                    src_ref=send.at[chunk, d, size], dst_ref=recv.at[chunk, me, size], send_sem=send_sem.at[chunk],
                    recv_sem=recv_sem.at[chunk], device_id=(grp, z * 2 + pc), device_id_type=MESH,
                ).start()

            unless(first, near)
            far = jnp.where(pc == 0, far_planes[0], far_planes[1])
            pltpu.make_async_remote_copy(
                src_ref=send.at[chunk, PLANE + d, size], dst_ref=recv.at[chunk, PLANE + me, size],
                send_sem=send_sem.at[chunk], recv_sem=recv_sem.at[chunk], device_id=(grp, far * 2 + pc),
                device_id_type=MESH,
            ).start()

        each_peer(one)
        own_rows(chunk).start()

    def own_rows(chunk):
        size = pl.ds(0, SIZES[chunk])
        return pltpu.make_async_copy(send.at[chunk, me, size], recv.at[chunk, me, size], self_sem.at[chunk])

    def wait_rows(ref, chunk, sem):
        part = ref.at[chunk, pl.ds(0, PEERS - 1), pl.ds(0, SIZES[chunk])]
        pltpu.make_async_copy(part, part, sem.at[chunk]).wait()

    def wait_blocks(ref, count, sem):
        pltpu.make_async_copy(ref.at[pl.ds(0, count)], ref.at[pl.ds(0, count)], sem).wait()

    def take_rows(chunk):
        wait_rows(recv, chunk, recv_sem)
        own_rows(chunk).wait()
        group, size = 2 * CHUNKS[chunk][1], SIZES[chunk]
        used = DEPTH * group
        tail = used // 8 * 8
        live = lax.broadcasted_iota(jnp.int32, (size, RANK), 0) < used

        def sixteen(part, carry):
            total = jnp.zeros((size - tail, RANK), jnp.float32)
            for index in range(16):
                source = part * 16 + index
                block = recv[chunk, source, pl.ds(0, size)].astype(jnp.float32)
                flat[pl.ds(pl.multiple_of(source * size, size), size), :] = jnp.where(live, block, 0.0)
                total = total + block[tail:]
            conf_parts[part, pl.ds(0, size - tail)] = total
            return carry

        lax.fori_loop(0, PEERS // 16, sixteen, 0)
        for part in range(PEERS // 16):
            at = pl.ds(part * RANK, RANK)
            conf_all[chunk, pl.ds(0, group), at] = conf_parts[part, pl.ds(used - tail, group)]
        values = conf_all[chunk]
        weight = (1.0 + values).astype(jnp.bfloat16).astype(jnp.float32)
        weight_all[chunk] = jnp.where(values > 0.0, weight, 0.0)

    def own_gram():
        gram_own[...] = jnp.zeros_like(gram_own)

        def one_block(block, carry):
            part = users[pl.ds(pl.multiple_of(block * 512, 512), 512), :]
            gram_own[...] += lax.dot_general(part, part, (((0,), (0,)), ((), ())), preferred_element_type=jnp.float32)
            return carry

        lax.fori_loop(0, USERS // 512, one_block, 0)
        for index in range(PLANE):
            gram_cut[index] = gram_own[pl.ds(index * PIECE, PIECE), :]

    def post_gram():
        def one(grp, pc, d, first):
            def start_copy():
                pltpu.make_async_remote_copy(
                    src_ref=gram_cut.at[d], dst_ref=gram_parts.at[me], send_sem=part_sem.at[0],
                    recv_sem=part_sem.at[1], device_id=(grp, z * 2 + pc), device_id_type=MESH,
                ).start()

            unless(first, start_copy)

        each_peer(one)
        gram_parts[me] = gram_cut[me]

    def pair_copy():
        return pltpu.make_async_remote_copy(
            src_ref=piece_send.at[0], dst_ref=piece_recv.at[0], send_sem=piece_send_sem.at[0],
            recv_sem=piece_recv_sem.at[0], device_id=(lax.axis_index("grp"), far_plane * 2 + core), device_id_type=MESH,
        )

    def next_copy():
        return pltpu.make_async_remote_copy(
            src_ref=piece_send.at[1], dst_ref=piece_recv.at[1], send_sem=piece_send_sem.at[1],
            recv_sem=piece_recv_sem.at[1], device_id=along(2), device_id_type=MESH,
        )

    def round_copy(turn, down):
        at = 2 + 4 * down + turn
        return pltpu.make_async_remote_copy(
            src_ref=piece_send.at[2] if turn == 0 else piece_recv.at[at - 1], dst_ref=piece_recv.at[at],
            send_sem=piece_send_sem.at[at], recv_sem=piece_recv_sem.at[at], device_id=along(-4 if down else 4),
            device_id_type=MESH,
        )

    def pair_turn():
        wait_blocks(gram_parts, PLANE - 1, part_sem.at[1])
        piece_send[0] = jnp.sum(gram_parts[...], axis=0)
        pair_copy().start()

    def next_turn():
        pair_copy().wait_recv()
        piece_send[1] = piece_send[0] + piece_recv[0]
        next_copy().start()

    def round_turn(turn):
        if turn == 0:
            next_copy().wait_recv()
            piece_send[2] = piece_send[1] + piece_recv[1]
        else:
            round_copy(turn - 1, 0).wait_recv()
            if turn < 4:
                round_copy(turn - 1, 1).wait_recv()
        if turn < 4:
            round_copy(turn, 0).start()
        if turn < 3:
            round_copy(turn, 1).start()

    def post_total():
        total = jnp.sum(piece_recv[pl.ds(2, 7)], axis=0) + piece_send[2]
        gram_piece[...] = total

        def one(grp, pc, d, first):
            def start_copy():
                pltpu.make_async_remote_copy(
                    src_ref=gram_piece, dst_ref=gram_all.at[me], send_sem=all_sem.at[0],
                    recv_sem=all_sem.at[1], device_id=(grp, z * 2 + pc), device_id_type=MESH,
                ).start()

            unless(first, start_copy)

        each_peer(one)
        gram_all[me] = total

    def beside(step):
        if step == 0:
            next_turn()
        elif step < 6:
            round_turn(step - 1)
        if step == 5:
            post_total()

    def item_gram(into, chunk, index):
        values = flat[pl.ds(index, LENGTH, stride=2 * CHUNKS[chunk][1]), :]
        scaled = (jnp.transpose(values) * conf_all[chunk, pl.ds(index, 1), :]).astype(jnp.bfloat16)
        weights = jnp.broadcast_to(weight_all[chunk, pl.ds(index, 1), :], (16, LENGTH)).astype(jnp.bfloat16)
        left = jnp.concatenate([scaled, weights], axis=0)
        product = jnp.dot(left, values.astype(jnp.bfloat16), preferred_element_type=jnp.float32)
        into[...] = product[:UNIT]

    def up_copy(step, part):
        first, count = CUTS[part]
        at = pl.ds(first, count)
        return pltpu.make_async_remote_copy(
            src_ref=up_send.at[step, at], dst_ref=up_recv.at[step, at], send_sem=up_send_sem.at[step, part],
            recv_sem=up_recv_sem.at[step, part], device_id=along(2), device_id_type=MESH,
        )

    def down_copy(step, part):
        first, count = CUTS[part]
        at = pl.ds(first, count)
        return pltpu.make_async_remote_copy(
            src_ref=down_send.at[step, at], dst_ref=down_recv.at[step, at], send_sem=down_send_sem.at[step, part],
            recv_sem=down_recv_sem.at[step, part], device_id=along(-2), device_id_type=MESH,
        )

    stage[...] = jnp.zeros_like(stage)
    spread_conf()
    gather(0)
    pl.semaphore_wait(barrier, PLANE - 1 + PLANE + 4)
    post_rows(0)
    own_gram()
    post_gram()
    for chunk in range(1, AHEAD):
        gather(chunk)
        post_rows(chunk)

    def chain(step, chunk):
        index = (step - CHUNKS[chunk][0]) * 2
        item_gram(up_send.at[step], chunk, index)
        item_gram(down_send.at[step], chunk, index + 1)
        for part, (begin, count) in enumerate(CUTS):
            at = pl.ds(begin, count)
            if step > 0:
                up_copy(step - 1, part).wait_recv()
                up_send[step, at] += up_recv[step - 1, at]
            up_copy(step, part).start()
            if step > 0:
                down_copy(step - 1, part).wait_recv()
                down_send[step, at] += down_recv[step - 1, at]
            if step < STEPS - 1:
                down_copy(step, part).start()
        if AHEAD + step < len(CHUNKS):
            gather(AHEAD + step)
            post_rows(AHEAD + step)
        beside(step)

    for chunk, (first, count) in enumerate(CHUNKS):
        if chunk == 0:
            pair_turn()
        take_rows(chunk)
        for step in range(first, first + count):
            chain(step, chunk)
    row = lax.broadcasted_iota(jnp.int32, (RANK, RANK), 0)
    col = lax.broadcasted_iota(jnp.int32, (RANK, RANK), 1)
    wait_blocks(gram_all, PLANE - 1, all_sem.at[1])
    for index in range(PLANE):
        gram_own[pl.ds(index * PIECE, PIECE), :] = gram_all[index]
    gram_own[...] += down_send[STEPS - 1, pl.ds(0, RANK)] + jnp.where(row == col, RIDGE, 0.0)
    for part in range(len(CUTS)):
        up_copy(STEPS - 1, part).wait_recv()
    system = gram_own[...] + up_recv[STEPS - 1, pl.ds(0, RANK)]
    rhs = down_send[STEPS - 1, pl.ds(RANK, 1)] + up_recv[STEPS - 1, pl.ds(RANK, 1)]
    out[0] = solve(system, rhs, start[0])

    for chunk in range(len(CHUNKS)):
        wait_rows(send, chunk, send_sem)
    wait_blocks(gram_parts, PLANE - 1, part_sem.at[0])
    pair_copy().wait_send()
    next_copy().wait_send()
    for turn in range(4):
        round_copy(turn, 0).wait_send()
    for turn in range(3):
        round_copy(turn, 1).wait_send()
    wait_blocks(gram_all, PLANE - 1, all_sem.at[0])

    def drain(step, carry):
        for part in range(len(CUTS)):
            up_copy(step, part).wait_send()

            @pl.when(step < STEPS - 1)
            def _():
                down_copy(step, part).wait_send()

        return carry

    lax.fori_loop(0, STEPS, drain, 0)


def on_device(user_factors, user_rows, row_counts, confidence, slot_items, prev_factors):
    conf = confidence.reshape(WINDOW, DEPTH)
    live = lax.broadcasted_iota(jnp.int32, (WINDOW, DEPTH), 1) < row_counts[:, None]
    conf = jnp.pad(jnp.where(live, conf, jnp.zeros_like(conf)), ((0, 0), (0, 8 - DEPTH)))
    vmem = pl.BlockSpec(memory_space=pltpu.VMEM)
    smem = pl.BlockSpec(memory_space=pltpu.SMEM)
    f32, bf16 = jnp.float32, jnp.bfloat16
    dma = pltpu.SemaphoreType.DMA
    parts, chunks = len(CUTS), len(CHUNKS)
    return pl.pallas_call(
        kernel,
        out_shape=jax.ShapeDtypeStruct((1, 1, RANK), f32),
        in_specs=[smem, smem, vmem, vmem, vmem],
        out_specs=vmem,
        scratch_shapes=[
            pltpu.VMEM((USERS, RANK), f32),
            pltpu.VMEM((PEERS * max(SIZES), RANK), f32),
            pltpu.VMEM((len(CHUNKS), PEERS, max(SIZES), RANK), bf16),
            pltpu.VMEM((len(CHUNKS), PEERS, max(SIZES), RANK), bf16),
            pltpu.VMEM((PEERS * max(SIZES), RANK), f32),
            pltpu.VMEM((WINDOW, RANK), f32),
            pltpu.VMEM((PEERS // 16, 16, RANK), f32),
            pltpu.VMEM((len(CHUNKS), 8, LENGTH), f32),
            pltpu.VMEM((len(CHUNKS), 8, LENGTH), f32),
            pltpu.VMEM((RANK, RANK), f32),
            pltpu.VMEM((PLANE, PIECE, RANK), f32),
            pltpu.VMEM((PLANE, PIECE, RANK), f32),
            pltpu.VMEM((PIECE, RANK), f32),
            pltpu.VMEM((PLANE, PIECE, RANK), f32),
            pltpu.VMEM((3, PIECE, RANK), f32),
            pltpu.VMEM((9, PIECE, RANK), f32),
            pltpu.VMEM((STEPS, UNIT, RANK), f32),
            pltpu.VMEM((STEPS, UNIT, RANK), f32),
            pltpu.VMEM((STEPS, UNIT, RANK), f32),
            pltpu.VMEM((STEPS, UNIT, RANK), f32),
            dma((chunks,)), dma((chunks,)), dma((chunks,)), dma((2,)), dma((2,)), dma((9,)), dma((9,)),
            dma((STEPS, parts)), dma((STEPS, parts)), dma((STEPS, parts)), dma((STEPS, parts)),
        ],
        compiler_params=pltpu.CompilerParams(
            collective_id=0, has_side_effects=True, vmem_limit_bytes=48 * 1024 * 1024
        ),
    )(slot_items, user_rows, conf, user_factors, prev_factors)


def solution(mesh):
    in_specs = (
        P(("grp", "own"), None),
        P(("grp", "own")),
        P(("grp", "own")),
        P(("grp", "own")),
        P(),
        P("own", "grp", None),
    )
    out_specs = P("own", "grp", None)
    return jax.shard_map(
        on_device, mesh=mesh, in_specs=in_specs, out_specs=out_specs, check_vma=False
    )
```
